128 devices in a mesh: dp: 16 (over y, z_hi, core), seq: 8 (over x, z_lo).
Axes of the slice: x: 4, y: 4, z: 4 (z_hi: 2, z_lo: 2; z = z_hi * 2 + z_lo), core: 2. Of those that a mesh axis runs over, the one named last changes fastest.
Arguments:
- tokens: bfloat16 [16, 2048, 1024], P('dp', 'seq'), may hold values from -6 to 6
- proj_weight: bfloat16 [1024, 4096], replicated, may hold values from -0.1875 to 0.1875
- out_weight: bfloat16 [1024, 1024], replicated, may hold values from -0.1875 to 0.1875
- rel_bias: float32 [8, 128], replicated, may hold values from -4 to 4
- segment_ids: int32 [16, 2048], P('dp'), may hold values from 0 to 3, never falling along the last dimension, each value on 1 to 1024 neighbouring positions
- distance_bucket: int32 [2048], replicated, may hold values from 0 to 127
- out_grad: bfloat16 [16, 2048, 1024], P('dp', 'seq'), may hold values from -6 to 6
Outputs:
- layer_out: bfloat16 [16, 2048, 1024], P('dp', 'seq')
- input_grad: bfloat16 [16, 2048, 1024], P('dp', 'seq')
- proj_grad: float32 [1024, 4096], P(('dp', 'seq'))
- out_weight_grad: float32 [1024, 1024], P(('dp', 'seq'))
The draws below stay inside these ranges and needn't reach their ends.
Inputs may be any that keep to these rules, and one draw needn't show every extreme that they name: `segment_ids`: ids never fall along a row; each history is 1 to 1024 positions long, and one history of every row has exactly 1024 positions.
All inputs are finite; a program needn't handle non-finite values.
Results may differ from the reference program's by a relative error of at most 0.0095.
Values may be sent and summed in bfloat16 or wider, within the bound.
No kernel may reach another device: no remote copies, remote signals or barrier semaphores. Data moves between devices by JAX's collectives and lax.ppermute only.
A program may use at most 704 MiB of HBM per device.

```python
import math
import jax
import jax.numpy as jnp
import numpy as np
from jax import lax

D = 1024
H = 8
HD = 128
NB = 128
HISTS = 4
L = 2048
HIST_MOST = 1024
PROJ = 4096
N_DP = 16


def set_ends(array, stream_key, low, high):
    dims = array.shape
    place = [jax.random.randint(jax.random.fold_in(stream_key, axis), (), 0, dims[axis]) for axis in range(len(dims))]
    array = array.at[tuple(place)].set(low)
    longest = dims.index(max(dims))
    place[longest] = (place[longest] + 1) % dims[longest]
    return array.at[tuple(place)].set(high)


def spiked(drawn, key, source, target, blocks, factor):
    owner, partner = [(jnp.arange(drawn.shape[position]) // (drawn.shape[position] // blocks)).reshape([-1 if axis == position else 1 for axis in range(drawn.ndim)]) for position in (source, target)]
    chosen = jax.random.permutation(key, blocks)[partner]
    strong = (owner == chosen) | (owner == (partner + blocks // 2) % blocks)
    return jnp.where(strong, factor * drawn, drawn)


def levels(key, extent, cuts, smallest, high):
    factor_of = 1.0
    for dim, blocks in cuts:
        steps = jax.random.uniform(jax.random.fold_in(jax.random.fold_in(key, 6), dim), (blocks,), jnp.float32, smallest / len(cuts), high / len(cuts))
        factor_of = factor_of * jnp.repeat(jnp.exp(steps), extent[dim] // blocks).reshape((-1,) + (1,) * (len(extent) - 1 - dim))
    return factor_of


def split_up(number_of, total, reach, slope):
    weights = [(1 << 20) // math.isqrt(grade ** slope) + 1 for grade in range(2, number_of + 1)]
    spare, counts = total - reach - (number_of - 1), [1] * (number_of - 1)
    while spare > 0:
        movable = [i for i in range(number_of - 1) if counts[i] < reach]
        pool, budget = sum([weights[i] for i in movable]), spare
        for i in movable:
            addition = min(reach - counts[i], max(1, budget * weights[i] // pool), spare)
            counts[i] = counts[i] + addition
            spare = spare - addition
    return np.array([reach] + counts)


def uneven(key, count, total, limit, slope):
    if count == 2:
        one = jax.random.randint(key, (), max(1, total - limit), min(limit, total - 1) + 1)
        return jnp.stack([one, total - one])
    lengths = jnp.asarray(split_up(count, total, limit, slope), jnp.int32)
    twos = (count - 1) // 2
    source_of, receiver = lengths[1:1 + 2 * twos:2], lengths[2:2 + 2 * twos:2]
    margin = jnp.minimum(source_of - 1, limit - receiver)
    moved = jax.random.randint(jax.random.fold_in(key, 1), (twos,), 0, 1 << 20) % (margin + 1)
    lengths = lengths.at[1:1 + 2 * twos:2].set(source_of - moved).at[2:2 + 2 * twos:2].set(receiver + moved)
    return lengths[jax.random.permutation(jax.random.fold_in(key, 2), count)]


def gaussian(key, shape, spread, limit, shards=(), kind=jnp.bfloat16):
    values = spread * jax.random.normal(key, shape, jnp.float32)
    if shards:
        values = values * levels(key, shape, shards, -0.22, 0.18)
    return jnp.clip(values, -limit, limit).astype(kind)


def heavy_noise(key, extent, spread, limit, shards, heavy, kind=jnp.bfloat16):
    entries = spread * jax.random.normal(key, extent, jnp.float32)
    if shards:
        entries = entries * levels(key, extent, shards, -0.22, 0.18)
    return jnp.clip(spiked(entries, jax.random.fold_in(key, 3), *heavy), -limit, limit).astype(kind)


def setup_inputs(seed: int = 0) -> dict:
    key_of = jax.random.split(jax.random.key(seed), 8)
    return {
        "tokens": heavy_noise(key_of[0], (N_DP, L, D), 1.0, 6.0, ((0, 16), (1, 8)), (1, 2, 8, 2.0)),
        "proj_weight": gaussian(key_of[1], (D, PROJ), D ** -0.5, 0.1875),
        "out_weight": gaussian(key_of[2], (D, D), D ** -0.5, 0.1875),
        "rel_bias": gaussian(key_of[3], (H, NB), 1.0, 4.0, (), jnp.float32),
        "segment_ids": jax.vmap(lambda own: jnp.searchsorted(jnp.cumsum(uneven(own, HISTS, L, HIST_MOST, 2)), jnp.arange(L), side="right"))(jax.random.split(key_of[4], N_DP)).reshape((N_DP, L)).astype(jnp.int32),
        "distance_bucket": set_ends(jax.random.randint(key_of[5], (L,), 0, NB), jax.random.fold_in(key_of[5], 1), 0, NB - 1).astype(jnp.int32),
        "out_grad": gaussian(key_of[6], (N_DP, L, D), 1.0, 6.0, ((0, 16), (1, 8))),
    }


def layer_norm(values):
    average = lax.optimization_barrier(jnp.mean(values, axis=-1, keepdims=True))
    centered = values - average
    inverse = lax.rsqrt(lax.optimization_barrier(jnp.mean(centered * centered, axis=-1, keepdims=True)) + 1e-05)
    return (centered * inverse, inverse)

def norm_back(upstream, normed, inverse):
    first = lax.optimization_barrier(jnp.mean(upstream, axis=-1, keepdims=True))
    second = lax.optimization_barrier(jnp.mean(upstream * normed, axis=-1, keepdims=True))
    return (upstream - first - normed * second) * inverse

def silu_slope(values):
    sigmoid_of = jax.nn.sigmoid(values)
    return sigmoid_of * (1.0 + values * (1.0 - sigmoid_of))

def reference(tokens, proj_weight, out_weight, rel_bias, segment_ids, distance_bucket, out_grad):
    highest = lax.Precision.HIGHEST
    score_scale = HD ** (-0.5)
    bias_table = rel_bias[:, distance_bucket]
    positions = jnp.arange(L, dtype=jnp.int32)
    gaps = positions[:, None] - positions[None, :]
    full_bias = bias_table[:, jnp.clip(gaps, 0, L - 1)]

    def row_step(running, inputs):
        token_row, segment_row, upstream = inputs
        normed, x_inverse = layer_norm(token_row.astype(jnp.float32))
        normed_half = normed.astype(jnp.bfloat16)
        projected = jnp.dot(normed_half, proj_weight, preferred_element_type=jnp.float32)
        features = jax.nn.silu(projected).astype(jnp.bfloat16)
        gate_part, value, query, key = jnp.split(features, 4, axis=1)
        query_heads = query.astype(jnp.float32).reshape(L, H, HD)
        key_heads = key.astype(jnp.float32).reshape(L, H, HD)
        value_heads = value.astype(jnp.float32).reshape(L, H, HD)
        live = (gaps >= 0) & (segment_row[:, None] == segment_row[None, :])
        scores = jnp.einsum('ihd,jhd->hij', query_heads, key_heads, precision=highest) * score_scale + full_bias
        weights = jnp.where(live, jax.nn.silu(scores), 0.0).astype(jnp.bfloat16)
        weights_wide = weights.astype(jnp.float32)
        attended = jnp.einsum('hij,jhd->ihd', weights_wide, value_heads, precision=highest).reshape(L, D)
        mixed_norm, y_inverse = layer_norm(attended)
        gate_wide = gate_part.astype(jnp.float32)
        gated = (mixed_norm * gate_wide).astype(jnp.bfloat16)
        layer_row = (token_row.astype(jnp.float32) + jnp.dot(gated, out_weight, preferred_element_type=jnp.float32)).astype(jnp.bfloat16)
        grad_gated = jnp.dot(upstream, out_weight.T, preferred_element_type=jnp.float32)
        grad_gate = grad_gated * mixed_norm
        grad_attended = norm_back(grad_gated * gate_wide, mixed_norm, y_inverse).astype(jnp.bfloat16)
        grad_heads = grad_attended.astype(jnp.float32).reshape(L, H, HD)
        grad_weights = jnp.einsum('ihd,jhd->hij', grad_heads, value_heads, precision=highest)
        grad_scores = jnp.where(live, grad_weights * silu_slope(scores), 0.0).astype(jnp.bfloat16)
        scores_wide = grad_scores.astype(jnp.float32)
        grad_query = jnp.einsum('hij,jhd->ihd', scores_wide, key_heads, precision=highest) * score_scale
        grad_key = jnp.einsum('hij,ihd->jhd', scores_wide, query_heads, precision=highest) * score_scale
        grad_value = jnp.einsum('hij,ihd->jhd', weights_wide, grad_heads, precision=highest)
        grad_features = jnp.concatenate([grad_gate, grad_value.reshape(L, D), grad_query.reshape(L, D), grad_key.reshape(L, D)], axis=1)
        grad_projected = (grad_features * silu_slope(projected)).astype(jnp.bfloat16)
        grad_normed = jnp.dot(grad_projected, proj_weight.T, preferred_element_type=jnp.float32)
        grad_row = (upstream.astype(jnp.float32) + norm_back(grad_normed, normed, x_inverse)).astype(jnp.bfloat16)
        term_in = jnp.dot(normed_half.T, grad_projected, preferred_element_type=jnp.float32)
        term_out = jnp.dot(gated.T, upstream, preferred_element_type=jnp.float32)
        return (running + jnp.concatenate([term_in, term_out], axis=1), (layer_row, grad_row))
    start_sum = jnp.zeros((D, 5 * D), jnp.float32)
    summed, (layer_out, input_grad) = lax.scan(row_step, start_sum, (tokens, segment_ids, out_grad))
    return (layer_out, input_grad, summed[:, :4 * D], summed[:, 4 * D:])
```

```python
import functools
import jax
import jax.numpy as jnp
from jax import lax
from jax.experimental import pallas as pl
from jax.experimental.pallas import tpu as pltpu
from jax.sharding import PartitionSpec as P

EPS = 1e-05
TILE = 256
DEAD = -1e30
F32 = jnp.float32
BF16 = jnp.bfloat16
VMEM_BYTES = 48 * 1024 * 1024


def sigmoid_of(values):
    return 0.5 * jnp.tanh(0.5 * values) + 0.5


def silu(values):
    return values * sigmoid_of(values)


def silu_slope(values):
    sig = sigmoid_of(values)
    return sig * (1.0 + values * (1.0 - sig))


def layer_norm(values):
    average = jnp.mean(values, axis=-1, keepdims=True)
    centered = values - average
    inverse = lax.rsqrt(jnp.mean(centered * centered, axis=-1, keepdims=True) + EPS)
    return centered * inverse, inverse


def dot_nn(left, right):
    return lax.dot_general(left, right, (((1,), (0,)), ((), ())), preferred_element_type=F32)


def dot_nt(left, right):
    return lax.dot_general(left, right, (((1,), (1,)), ((), ())), preferred_element_type=F32)


def dot_tn(left, right):
    return lax.dot_general(left, right, (((0,), (0,)), ((), ())), preferred_element_type=F32)


def whole(memory_space=pltpu.VMEM):
    return pl.BlockSpec(memory_space=memory_space)


def call(kernel, outs, name, smem=0, scratch=(), flops=0):
    def run(*args):
        size = sum(a.size * a.dtype.itemsize for a in args)
        size += sum(o.size * o.dtype.itemsize for o in outs)
        return pl.pallas_call(
            kernel,
            out_shape=outs,
            in_specs=[whole(pltpu.SMEM)] * smem + [whole()] * (len(args) - smem),
            out_specs=[whole()] * len(outs),
            scratch_shapes=list(scratch),
            compiler_params=pltpu.CompilerParams(vmem_limit_bytes=VMEM_BYTES),
            cost_estimate=pl.CostEstimate(flops=flops, bytes_accessed=size, transcendentals=0),
            name=name,
        )(*args)

    return run


def shape(dims, kind):
    return jax.ShapeDtypeStruct(dims, kind)


def norm_kernel(token_ref, half_ref):
    normed, _ = layer_norm(token_ref[...].astype(F32))
    half_ref[...] = normed.astype(BF16)


def owner_kernel(up_ref, out_w_ref, half_ref, gate_w_ref, gg_ref, split_ref, gate_ref):
    gg = dot_nt(up_ref[...], out_w_ref[...])
    gg_ref[...] = gg
    head_size = split_ref.shape[2]
    for head in range(split_ref.shape[0]):
        split_ref[head] = gg[:, head * head_size : (head + 1) * head_size].astype(BF16)
    gate_ref[...] = dot_nn(half_ref[...], gate_w_ref[...])


def bias_kernel(table_ref, tile_ref):
    count = tile_ref.shape[0]
    key_at = lax.broadcasted_iota(jnp.int32, (TILE, TILE), 0)
    query_at = lax.broadcasted_iota(jnp.int32, (TILE, TILE), 1)
    for step in range(count):
        if step < count - 1:
            later = table_ref[:, step * TILE : (step + 1) * TILE]
        else:
            later = jnp.zeros((1, TILE), F32)
        if step > 0:
            earlier = table_ref[:, (step - 1) * TILE : step * TILE]
        else:
            earlier = jnp.zeros((1, TILE), F32)
        window = jnp.broadcast_to(jnp.concatenate([later, earlier], axis=1), (TILE, 2 * TILE))
        rolled = pltpu.roll(window, 0, 1, stride=1, stride_axis=0)[:, :TILE]
        if step == 0:
            rolled = jnp.where(key_at <= query_at, rolled, DEAD)
        tile_ref[step] = rolled


def first_block(segment_smem, query_block, reach):
    first_segment = segment_smem[0, query_block * TILE]
    count = 0
    for back in range(1, min(reach, query_block) + 1):
        last_key = (query_block - back + 1) * TILE - 1
        count = count + (segment_smem[0, last_key] == first_segment).astype(jnp.int32)
    return query_block - count


def forward_kernel(scale, offset_smem, segment_smem, *refs):
    blocks = refs[:8]
    weight_ref, bias_ref, column_ref, row_ref, gg_ref = refs[8:13]
    proj_ref, feature_ref, attended_ref, stat_ref = refs[13:]
    head = attended_ref.shape[1]
    count = attended_ref.shape[0] // TILE
    reach = bias_ref.shape[0] - 1
    for block, ref in enumerate(blocks):
        start = pl.multiple_of(offset_smem[block], TILE)
        projected = dot_nn(ref[...], weight_ref[...])
        proj_ref[pl.ds(start, TILE), :] = projected
        feature_ref[pl.ds(start, TILE), :] = silu(projected).astype(BF16)
    lane = lax.broadcasted_iota(jnp.int32, (TILE, head), 1)
    for q_block in range(count):
        rows = pl.ds(q_block * TILE, TILE)
        query = feature_ref[rows, 2 * head : 3 * head]
        q_segment = row_ref[:, q_block * TILE : (q_block + 1) * TILE]

        def step(k_block, total):
            k_rows = pl.ds(pl.multiple_of(k_block * TILE, TILE), TILE)
            key = feature_ref[k_rows, 3 * head : 4 * head]
            value = feature_ref[k_rows, head : 2 * head]
            score = dot_nt(key, query) * scale + bias_ref[q_block - k_block]
            score = jnp.where(column_ref[k_rows, 0:1] == q_segment, score, DEAD)
            weight = silu(score).astype(BF16)
            return total + dot_tn(weight, value)

        attended = lax.fori_loop(
            first_block(segment_smem, q_block, reach), q_block + 1, step, jnp.zeros((TILE, head), F32)
        )
        attended_ref[rows, :] = attended
        gate = feature_ref[rows, :head].astype(F32)
        grad = gg_ref[rows, :].astype(F32) * gate
        total = jnp.sum(attended, axis=1, keepdims=True)
        centered = attended - total * (1.0 / head)
        spread = jnp.sum(centered * centered, axis=1, keepdims=True)
        grad_sum = jnp.sum(grad, axis=1, keepdims=True)
        cross = jnp.sum(grad * centered, axis=1, keepdims=True)
        packed = jnp.where(
            lane == 0, total, jnp.where(lane == 1, spread, jnp.where(lane == 2, grad_sum, cross))
        )
        half = q_block * 2 // count
        start = (q_block - half * (count // 2)) * TILE
        stat_ref[half * 4 : half * 4 + 4, start : start + TILE] = packed.T[0:4, :]


def mix_kernel(stat_ref, attended_ref, proj_ref, gg_ref, norm_ref, grad_ref, gate_grad_ref):
    head = attended_ref.shape[1]
    heads = stat_ref.shape[0]
    width = head * heads
    span = stat_ref.shape[2]
    for half in range(2):
        total = stat_ref[:, half * 4, :]
        spread = stat_ref[:, half * 4 + 1, :]
        grad_sum = stat_ref[:, half * 4 + 2, :]
        cross = stat_ref[:, half * 4 + 3, :]
        own = total * (1.0 / head)
        average = jnp.sum(total, axis=0, keepdims=True) * (1.0 / width)
        apart = own - average
        variance = jnp.sum(spread + head * apart * apart, axis=0, keepdims=True) * (1.0 / width)
        inverse = lax.rsqrt(variance + EPS)
        first = jnp.sum(grad_sum, axis=0, keepdims=True) * (1.0 / width)
        second = jnp.sum(cross + grad_sum * apart, axis=0, keepdims=True) * inverse * (1.0 / width)
        rows = jnp.concatenate(
            [average, inverse, first, second, jnp.zeros((4, span), F32)], axis=0
        )
        columns = rows.T
        for block in range(span // TILE):
            here = slice(block * TILE, (block + 1) * TILE)
            there = pl.ds(half * span + block * TILE, TILE)
            average_c = columns[here, 0:1]
            inverse_c = columns[here, 1:2]
            first_c = columns[here, 2:3]
            second_c = columns[here, 3:4]
            mixed = (attended_ref[there, :] - average_c) * inverse_c
            norm_ref[there, :] = mixed.astype(BF16)
            projected = proj_ref[there, :head]
            gate = silu(projected).astype(BF16).astype(F32)
            gg = gg_ref[there, :].astype(F32)
            grad = (gg * gate - first_c - mixed * second_c) * inverse_c
            grad_ref[there, :] = grad.astype(BF16)
            gate_grad_ref[there, :] = (gg * mixed * silu_slope(projected)).astype(BF16)


def backward_kernel(
    scale, segment_smem, bias_ref, column_ref, row_ref, feature_ref, grad_ref, proj_ref, out_ref,
    key_sum, value_sum,
):
    head = grad_ref.shape[1]
    count = grad_ref.shape[0] // TILE
    reach = bias_ref.shape[0] - 1
    key_sum[...] = jnp.zeros_like(key_sum)
    value_sum[...] = jnp.zeros_like(value_sum)
    for q_block in range(count):
        rows = pl.ds(q_block * TILE, TILE)
        query = feature_ref[rows, 2 * head : 3 * head]
        upstream = grad_ref[rows, :]
        q_segment = row_ref[:, q_block * TILE : (q_block + 1) * TILE]

        def step(k_block, total):
            k_rows = pl.ds(pl.multiple_of(k_block * TILE, TILE), TILE)
            key = feature_ref[k_rows, 3 * head : 4 * head]
            value = feature_ref[k_rows, head : 2 * head]
            score = dot_nt(key, query) * scale + bias_ref[q_block - k_block]
            score = jnp.where(column_ref[k_rows, 0:1] == q_segment, score, DEAD)
            sig = sigmoid_of(score)
            weight = score * sig
            slope = sig + weight * (1.0 - sig)
            grad_weight = dot_nt(value, upstream)
            grad_score = (grad_weight * slope).astype(BF16)
            value_sum[k_rows, :] += dot_nn(weight.astype(BF16), upstream)
            key_sum[k_rows, :] += dot_nn(grad_score, query)
            return total + dot_tn(grad_score, key)

        total = lax.fori_loop(
            first_block(segment_smem, q_block, reach), q_block + 1, step, jnp.zeros((TILE, head), F32)
        )
        slope = silu_slope(proj_ref[rows, 2 * head : 3 * head])
        out_ref[rows, head : 2 * head] = (total * scale * slope).astype(BF16)
    for block in range(count):
        rows = pl.ds(block * TILE, TILE)
        value_slope = silu_slope(proj_ref[rows, head : 2 * head])
        key_slope = silu_slope(proj_ref[rows, 3 * head : 4 * head])
        out_ref[rows, :head] = (value_sum[rows, :] * value_slope).astype(BF16)
        out_ref[rows, 2 * head : 3 * head] = (key_sum[rows, :] * scale * key_slope).astype(BF16)


def weight_kernel(offset_smem, *refs):
    blocks = refs[:8]
    gate_grad_ref, grad_ref, out_ref = refs[8:]
    head = gate_grad_ref.shape[1]
    starts = [pl.multiple_of(offset_smem[block], TILE) for block in range(8)]
    for chunk in range(out_ref.shape[0] // TILE):
        columns = slice(chunk * TILE, (chunk + 1) * TILE)
        gate_part = 0.0
        rest = 0.0
        for block, ref in enumerate(blocks):
            rows = pl.ds(starts[block], TILE)
            gate_part += dot_tn(ref[:, columns], gate_grad_ref[rows, :])
            rest += dot_tn(ref[:, columns], grad_ref[rows, :])
        out_ref[columns, :head] = gate_part.astype(BF16)
        out_ref[columns, head:] = rest.astype(BF16)


def output_kernel(
    mixed_ref, gate_ref, gg_ref, token_ref, out_w_ref, up_ref, layer_ref, gate_grad_ref, sum_ref
):
    heads = mixed_ref.shape[0]
    mixed = jnp.concatenate([mixed_ref[head] for head in range(heads)], axis=1).astype(F32)
    projected = gate_ref[...]
    gate = silu(projected).astype(BF16).astype(F32)
    gated = (mixed * gate).astype(BF16)
    gate_grad_ref[...] = (gg_ref[...] * mixed * silu_slope(projected)).astype(BF16)
    layer_ref[...] = (token_ref[...].astype(F32) + dot_nn(gated, out_w_ref[...])).astype(BF16)
    sum_ref[...] = dot_tn(gated, up_ref[...]).astype(BF16)


def input_kernel(token_ref, up_ref, gate_grad_ref, grad_ref, weight_ref, out_ref, all_grad, total):
    step = pl.program_id(0)
    heads = grad_ref.shape[0]
    head = grad_ref.shape[2] // 3
    width = heads * head

    @pl.when(step == 0)
    def _():
        all_grad[:, :width] = gate_grad_ref[...]
        for index in range(heads):
            for part in range(3):
                start = (part + 1) * width + index * head
                all_grad[:, start : start + head] = grad_ref[index, :, part * head : (part + 1) * head]

    total[step] = dot_nt(all_grad[...], weight_ref[...])

    @pl.when(step == pl.num_programs(0) - 1)
    def _():
        grad = jnp.concatenate([total[index] for index in range(total.shape[0])], axis=1)
        normed, inverse = layer_norm(token_ref[...].astype(F32))
        first = jnp.mean(grad, axis=-1, keepdims=True)
        second = jnp.mean(grad * normed, axis=-1, keepdims=True)
        back = (grad - first - normed * second) * inverse
        out_ref[...] = (up_ref[...].astype(F32) + back).astype(BF16)


def input_grad_of(tokens, upstream, gate_grad, grads, weight):
    rows, width = tokens.shape
    steps = 4
    fixed = lambda *dims: pl.BlockSpec(dims, lambda step: (0,) * len(dims))
    return pl.pallas_call(
        input_kernel,
        grid=(steps,),
        out_shape=shape((rows, width), BF16),
        in_specs=[
            fixed(rows, width),
            fixed(rows, width),
            fixed(rows, width),
            fixed(*grads.shape),
            pl.BlockSpec((width // steps, weight.shape[1]), lambda step: (step, 0)),
        ],
        out_specs=fixed(rows, width),
        scratch_shapes=[
            pltpu.VMEM((rows, weight.shape[1]), BF16),
            pltpu.VMEM((steps, rows, width // steps), F32),
        ],
        compiler_params=pltpu.CompilerParams(vmem_limit_bytes=VMEM_BYTES),
        cost_estimate=pl.CostEstimate(
            flops=2 * rows * weight.size, bytes_accessed=2 * weight.size, transcendentals=0
        ),
        name="input_grad",
    )(tokens, upstream, gate_grad, grads, weight)


def shift(values, by):
    return lax.ppermute(values, "seq", [(index, (index + by) % 8) for index in range(8)])


def swap(values, axis, bits, size):
    return lax.ppermute(values, axis, [(index, index ^ bits) for index in range(size)])


def gather_blocks(own):
    mate = swap(own, "seq", 1, 8)
    after = shift(own, -2)
    before = shift(own, 2)
    mate_after = shift(mate, -2)
    mate_before = swap(before, "seq", 1, 8)
    across = shift(own, 4)
    mate_across = swap(across, "seq", 1, 8)
    me = lax.axis_index("seq")
    places = [me, me ^ 1, (me + 2) % 8, (me + 6) % 8]
    places += [(me ^ 1) + 2, (me ^ 1) + 6, me + 4, (me ^ 1) + 4]
    offsets = jnp.stack([(place % 8) * own.shape[0] for place in places]).astype(jnp.int32)
    return [own, mate, after, before, mate_after, mate_before, across, mate_across], offsets


def reduce_dp(partial):
    rows, columns = partial.shape
    cells = partial.reshape(8, 2, rows // 16, columns)
    place = lax.axis_index("dp")
    core = place % 2
    mine = lax.dynamic_index_in_dim(cells, core, 1, False)
    other = lax.dynamic_index_in_dim(cells, 1 - core, 1, False)
    other = swap(other, "dp", 1, 16)
    chip = (mine.astype(F32) + other.astype(F32)).astype(BF16)
    pair = place // 2
    total = lax.dynamic_index_in_dim(chip, pair, 0, False).astype(F32)
    for bits in range(1, 8):
        piece = lax.dynamic_index_in_dim(chip, pair ^ bits, 0, False)
        total = total + swap(piece, "dp", 2 * bits, 16).astype(F32)
    return total


def exchange(values):
    return lax.all_to_all(values, "seq", 0, 0)


def per_device(tokens, proj_weight, out_weight, rel_bias, segment_ids, distance_bucket, out_grad):
    heads, buckets = rel_bias.shape
    rows, width = tokens.shape[1:]
    head = width // heads
    length = segment_ids.shape[1]
    scale = head ** (-0.5)
    reach = 1024 // TILE
    me = lax.axis_index("seq")
    token_row = tokens[0]
    upstream = out_grad[0]

    half = call(norm_kernel, [shape((rows, width), BF16)], "norm")(token_row)[0]
    blocks, offsets = gather_blocks(half)

    gg, gg_split, gate_proj = call(
        owner_kernel,
        [shape((rows, width), F32), shape((heads, rows, head), BF16), shape((rows, width), F32)],
        "owner",
        flops=4 * rows * width * width,
    )(upstream, out_weight, half, proj_weight[:, :width])
    gg_head = exchange(gg_split).reshape(length, head)

    one_hot = (
        distance_bucket[None, : reach * TILE] == jnp.arange(buckets, dtype=jnp.int32)[:, None]
    ).astype(F32)
    table = jnp.dot(
        lax.dynamic_slice_in_dim(rel_bias, me, 1, 0),
        one_hot,
        precision=lax.Precision.HIGHEST,
        preferred_element_type=F32,
    )
    bias = call(bias_kernel, [shape((reach + 1, TILE, TILE), F32)], "bias")(table)[0]
    column = jnp.broadcast_to(segment_ids[0][:, None], (length, 128))
    weight = lax.dynamic_index_in_dim(
        proj_weight.reshape(width, 4, heads, head), me, 2, False
    ).reshape(width, 4 * head)

    projected, features, attended, stats = call(
        functools.partial(forward_kernel, scale),
        [
            shape((length, 4 * head), F32),
            shape((length, 4 * head), BF16),
            shape((length, head), F32),
            shape((8, length // 2), F32),
        ],
        "forward",
        smem=2,
        flops=2 * length * width * 4 * head,
    )(offsets, segment_ids, *blocks, weight, bias, column, segment_ids, gg_head)
    all_stats = exchange(jnp.broadcast_to(stats[None], (8,) + stats.shape))

    mixed, grad_attended, gate_grad = call(
        mix_kernel, [shape((length, head), BF16)] * 3, "mix"
    )(all_stats, attended, projected, gg_head)
    mixed_own = exchange(mixed.reshape(8, rows, head))

    grads = call(
        functools.partial(backward_kernel, scale),
        [shape((length, 3 * head), BF16)],
        "backward",
        smem=1,
        scratch=[pltpu.VMEM((length, head), F32)] * 2,
        flops=10 * length * 512 * head,
    )(segment_ids, bias, column, segment_ids, features, grad_attended, projected)[0]
    grads_own = exchange(grads.reshape(8, rows, 3 * head))

    layer_row, gate_grad_own, out_sum = call(
        output_kernel,
        [shape((rows, width), BF16), shape((rows, width), BF16), shape((width, width), BF16)],
        "output",
        flops=4 * rows * width * width,
    )(mixed_own, gate_proj, gg, token_row, out_weight, upstream)
    proj_sum = call(
        weight_kernel,
        [shape((width, 4 * head), BF16)],
        "weight",
        smem=1,
        flops=2 * length * width * 4 * head,
    )(offsets, *blocks, gate_grad, grads)[0]

    reduced = reduce_dp(jnp.concatenate([proj_sum, out_sum], axis=1))
    final = exchange(reduced.reshape(8, reduced.shape[0] // 8, reduced.shape[1]))
    few = final.shape[1]
    proj_out = final[:, :, : 4 * head].reshape(8, few, 4, head)
    proj_out = proj_out.transpose(1, 2, 0, 3).reshape(few, 4 * width)
    out_out = jnp.sum(final[:, :, 4 * head :], axis=0)

    grad_row = input_grad_of(token_row, upstream, gate_grad_own, grads_own, proj_weight)
    return layer_row[None], grad_row[None], proj_out, out_out


def solution(mesh):
    return jax.shard_map(
        per_device,
        mesh=mesh,
        in_specs=(P("dp", "seq", None), P(), P(), P(), P("dp", None), P(), P("dp", "seq", None)),
        out_specs=(
            P("dp", "seq", None),
            P("dp", "seq", None),
            P(("dp", "seq"), None),
            P(("dp", "seq"), None),
        ),
        check_vma=False,
    )
```

```python
import functools
import jax
import jax.numpy as jnp
from jax import lax
from jax.experimental import pallas as pl
from jax.experimental.pallas import tpu as pltpu
from jax.sharding import PartitionSpec as P

EPS = 1e-05
TILE = 256
DEAD = -1e30
F32 = jnp.float32
BF16 = jnp.bfloat16
VMEM_BYTES = 58 * 1024 * 1024


def layer_norm(values):
    average = jnp.mean(values, axis=-1, keepdims=True)
    centered = values - average
    inverse = lax.rsqrt(jnp.mean(centered * centered, axis=-1, keepdims=True) + EPS)
    return centered * inverse, inverse


def dot_nn(left, right):
    return lax.dot_general(left, right, (((1,), (0,)), ((), ())), preferred_element_type=F32)


def dot_nt(left, right):
    return lax.dot_general(left, right, (((1,), (1,)), ((), ())), preferred_element_type=F32)


def dot_tn(left, right):
    return lax.dot_general(left, right, (((0,), (0,)), ((), ())), preferred_element_type=F32)


class Incoming:
    def __init__(self, far, near, sems, first, parts):
        self.near = near
        self.size = near.shape[0] // parts
        self.copies = []
        for part in range(parts):
            rows = pl.ds(part * self.size, self.size)
            self.copies.append(
                pltpu.make_async_copy(far.at[rows], near.at[rows], sems.at[first + part])
            )
        self.pending = [True] * parts

    def start(self, part):
        if part < len(self.copies):
            self.copies[part].start()

    def wait(self, part):
        if part < len(self.copies) and self.pending[part]:
            self.copies[part].wait()
            self.pending[part] = False

    def ready(self):
        for part in range(len(self.copies)):
            self.wait(part)
        return self.near


class Outgoing:
    def __init__(self, near, far, sems, first, parts):
        self.ref = near
        size = near.shape[0] // parts
        self.copies = []
        for part in range(parts):
            rows = pl.ds(part * size, size)
            self.copies.append(
                pltpu.make_async_copy(near.at[rows], far.at[rows], sems.at[first + part])
            )
        self.sent = [False] * parts

    def send(self, part=None):
        if part is not None and len(self.copies) == 1:
            return
        for index, copy in enumerate(self.copies):
            if part in (None, index) and not self.sent[index]:
                copy.start()
                self.sent[index] = True

    def finish(self):
        for copy in self.copies:
            copy.wait()


def call(body, outs, name, smem=0, scratch=(), flops=0, far=(), parts=None, out_parts=None):
    parts = parts or {}
    out_parts = out_parts or {}

    def run(*args):
        size = sum(a.size * a.dtype.itemsize for a in args)
        size += sum(o.size * o.dtype.itemsize for o in outs)
        near_in = [i for i in range(smem, len(args)) if i not in far]
        counts = [parts.get(i, 1) for i in near_in]
        kept = [pltpu.VMEM(args[i].shape, args[i].dtype) for i in near_in]
        kept += [pltpu.VMEM(out.shape, out.dtype) for out in outs]
        out_counts = [out_parts.get(i, 1) for i in range(len(outs))]
        kept += [pltpu.SemaphoreType.DMA((sum(counts),)), pltpu.SemaphoreType.DMA((sum(out_counts),))]

        def kernel(*refs):
            ins, refs = refs[: len(args)], refs[len(args) :]
            far_outs, refs = refs[: len(outs)], refs[len(outs) :]
            near, refs = refs[: len(near_in)], refs[len(near_in) :]
            near_outs, refs = refs[: len(outs)], refs[len(outs) :]
            in_sems, out_sems, extra = refs[0], refs[1], refs[2:]
            values = list(ins)
            first = 0
            for place, ref, count in zip(near_in, near, counts):
                values[place] = Incoming(ins[place], ref, in_sems, first, count)
                first += count
            for part in range(max(counts)):
                for place in near_in:
                    values[place].start(part)
            results = []
            first = 0
            for ref, away, count in zip(near_outs, far_outs, out_counts):
                results.append(Outgoing(ref, away, out_sems, first, count))
                first += count
            body(*values, *results, *extra)
            for place in near_in:
                values[place].ready()
            for result in results:
                result.send()
            for result in results:
                result.finish()

        return pl.pallas_call(
            kernel,
            out_shape=outs,
            in_specs=[pl.BlockSpec(memory_space=pltpu.SMEM)] * smem
            + [pl.BlockSpec(memory_space=pltpu.HBM)] * (len(args) - smem),
            out_specs=[pl.BlockSpec(memory_space=pltpu.HBM)] * len(outs),
            scratch_shapes=kept + list(scratch),
            compiler_params=pltpu.CompilerParams(vmem_limit_bytes=VMEM_BYTES),
            cost_estimate=pl.CostEstimate(flops=flops, bytes_accessed=size, transcendentals=0),
            name=name,
        )(*args)

    return run


def shape(dims, kind):
    return jax.ShapeDtypeStruct(dims, kind)


def norm_kernel(token, half):
    for part in range(len(token.copies)):
        token.wait(part)
        rows = slice(part * token.size, (part + 1) * token.size)
        normed, _ = layer_norm(token.near[rows, :].astype(F32))
        half.ref[rows, :] = normed.astype(BF16)
        half.send(part)


def prepare_kernel(me_smem, up, half, out_w, weight_far, gg, gate, weight, gate_w, sems):
    width = gate_w.shape[0]
    head = weight.ref.shape[1] // 3
    copies = [pltpu.make_async_copy(weight_far.at[:, :width], gate_w, sems.at[0])]
    for part in range(3):
        start = pl.multiple_of((part + 1) * width + me_smem[0] * head, head)
        source = weight_far.at[:, pl.ds(start, head)]
        target = weight.ref.at[:, part * head : (part + 1) * head]
        copies.append(pltpu.make_async_copy(source, target, sems.at[part + 1]))
    for copy in copies:
        copy.start()
    gg.ref[...] = dot_nt(up.ready()[...], out_w.ready()[...])
    gg.send()
    copies[0].wait()
    gate.ref[...] = dot_nn(half.ready()[...], gate_w[...])
    gate.send()
    for copy in copies[1:]:
        copy.wait()


def bias_tiles(table_ref, tile_ref, turned):
    count = tile_ref.shape[0]
    key_at = lax.broadcasted_iota(jnp.int32, (TILE, TILE), 0)
    query_at = lax.broadcasted_iota(jnp.int32, (TILE, TILE), 1)
    for step in range(count):
        if step < count - 1:
            later = table_ref[:, step * TILE : (step + 1) * TILE]
        else:
            later = jnp.zeros((1, TILE), F32)
        if step > 0:
            earlier = table_ref[:, (step - 1) * TILE : step * TILE]
        else:
            earlier = jnp.zeros((1, TILE), F32)
        window = jnp.broadcast_to(jnp.concatenate([later, earlier], axis=1), (TILE, 2 * TILE))
        rolled = 0.5 * pltpu.roll(window, 0, 1, stride=1, stride_axis=0)[:, :TILE]
        if step == 0:
            rolled = jnp.where(key_at <= query_at, rolled, DEAD)
        tile_ref[step] = rolled if turned else rolled.T


def key_mask(mask):
    return ((1.0 - mask.astype(F32)) * DEAD).astype(BF16)


def forward_kernel(scale, start_smem, *refs):
    weight, table, mask = refs[:3]
    pieces = refs[3 : PIECES + 3]
    feature, slope, attended, bias_ref, key_ref = refs[PIECES + 3 :]
    feature_ref, slope_ref = feature.ref, slope.ref
    count, _, head = attended.ref.shape
    reach = bias_ref.shape[0] - 1
    row_at = lax.broadcasted_iota(jnp.int32, (16, HALF), 0)
    bias_tiles(table.ready(), bias_ref, False)
    mask_ref = mask.ready()
    key_ref[:, head:] = key_mask(mask_ref[...])
    weight_ref = weight.ready()
    for index, piece in enumerate(pieces):
        ref = piece.ready()
        rows = pl.ds(pl.multiple_of(start_smem[index], HALF), ref.shape[0])
        half = 0.5 * dot_nn(ref[...], weight_ref[...])
        lean = jnp.tanh(half)
        rise = 1.0 + lean
        made = (half * rise).astype(BF16)
        feature_ref[rows, :] = made
        key_ref[rows, :head] = made[:, 2 * head :]
        slope_ref[rows, :] = (0.5 * rise * (1.0 + half * (1.0 - lean))).astype(BF16)
    feature.send()
    slope.send()
    for q_block in range(count):
        rows = slice(q_block * TILE, (q_block + 1) * TILE)
        query = jnp.concatenate([feature_ref[rows, head : 2 * head], mask_ref[rows, :]], axis=1)
        total = jnp.zeros((TILE, head), F32)
        for k_block in range(max(0, q_block - reach), q_block + 1):
            k_rows = slice(k_block * TILE, (k_block + 1) * TILE)
            half = dot_nt(query, key_ref[k_rows, :]) * (0.5 * scale) + bias_ref[q_block - k_block]
            weights = half * (1.0 + jnp.tanh(half))
            total = total + dot_nn(weights.astype(BF16), feature_ref[k_rows, :head])
        average = jnp.mean(total, axis=1, keepdims=True)
        attended.ref[q_block, :TILE, :] = (total - average).astype(BF16)
        wide = jnp.broadcast_to(average, total.shape).T[:16, :]
        high = wide.astype(BF16).astype(F32)
        low = wide - high
        packed = jnp.where(row_at == 0, high[:, :HALF], high[:, HALF:])
        packed = jnp.where(row_at == 2, low[:, :HALF], packed)
        packed = jnp.where(row_at == 3, low[:, HALF:], packed)
        attended.ref[q_block, TILE:, :] = packed.astype(BF16)
        attended.send(q_block)


def split_cells(core, total, cell):
    low = [total[2 * k * cell : (2 * k + 1) * cell] for k in range(2)]
    high = [total[(2 * k + 1) * cell : (2 * k + 2) * cell] for k in range(2)]
    mine = [jnp.where(core == 0, x, y) for x, y in zip(low, high)]
    other = [jnp.where(core == 0, y, x) for x, y in zip(low, high)]
    return mine, other


def mix_kernel(
    core_smem, attended_in, gate_in, gg_in, up, out_w, token,
    send_out, gate_grad_out, mine_out, other_out, layer, gated_ref,
):
    attended_ref = attended_in.ready()
    send_ref = send_out.ref
    heads, _, head = attended_ref.shape
    rows = []
    for index in range(heads):
        packed = attended_ref[index, TILE:, :].astype(F32)
        rows.append(
            jnp.concatenate([packed[0:1] + packed[2:3], packed[1:2] + packed[3:4]], axis=1)
        )
    averages = jnp.concatenate(rows, axis=0).T
    attended = jnp.concatenate(
        [
            attended_ref[index, :TILE, :].astype(F32) + averages[:, index : index + 1]
            for index in range(heads)
        ],
        axis=1,
    )
    mixed, inverse = layer_norm(attended)
    half = 0.5 * gate_in.ready()[...]
    lean = jnp.tanh(half)
    rise = 1.0 + lean
    gate = (half * rise).astype(BF16).astype(F32)
    gg = gg_in.ready()[...]
    gated_ref[...] = (mixed * gate).astype(BF16)
    gate_grad = (gg * mixed * (0.5 * rise * (1.0 + half * (1.0 - lean)))).astype(BF16)
    gate_grad_out.ref[...] = gate_grad
    gate_grad_out.send()
    grad = gg * gate
    first = jnp.mean(grad, axis=-1, keepdims=True)
    second = jnp.mean(grad * mixed, axis=-1, keepdims=True)
    grad = ((grad - first - mixed * second) * inverse).astype(BF16)
    for index in range(heads):
        columns = slice(index * head, (index + 1) * head)
        send_ref[index, :, :head] = grad[:, columns]
        send_ref[index, :, head:] = gate_grad[:, columns]
    send_out.send()
    core = core_smem[0]
    up_rows = up.ready()[...]
    cell = TILE // 4
    slots = mine_out.ref.shape[0]
    few = cell // slots
    for chunk in range(gated_ref.shape[1] // TILE):
        total = dot_tn(gated_ref[:, chunk * TILE : (chunk + 1) * TILE], up_rows)
        both = split_cells(core, total, cell)
        for out, cells in zip((mine_out, other_out), both):
            for slot in range(slots):
                rows = slice(slot * few, (slot + 1) * few)
                packed = jnp.concatenate([part[rows] for part in cells], axis=0)
                out.ref[slot, chunk * 2 * few : (chunk + 1) * 2 * few, :] = packed.astype(BF16)
    other_out.send()
    mine_out.send()
    result = dot_nn(gated_ref[...], out_w.ready()[...])
    layer.ref[...] = (token.ready()[...].astype(F32) + result).astype(BF16)


def backward_kernel(
    scale, table, mask, feature, grad_in, slope_in, out, key_sum, value_sum, bias_ref, key_ref
):
    head = key_sum.shape[1]
    out_ref = out.ref
    bias_tiles(table.ready(), bias_ref, True)
    mask_ref, feature_ref = mask.near, feature.near
    grad_ref, slope_ref = grad_in.near, slope_in.near
    count = grad_ref.shape[0]
    reach = bias_ref.shape[0] - 1
    for q_block in range(count):
        rows = slice(q_block * TILE, (q_block + 1) * TILE)
        for source in (mask, feature, grad_in, slope_in):
            source.wait(q_block)
        key_ref[rows, :head] = feature_ref[rows, 2 * head :]
        key_ref[rows, head:] = key_mask(mask_ref[rows, :])
        query_half = feature_ref[rows, head : 2 * head]
        query = jnp.concatenate([query_half, mask_ref[rows, :]], axis=1)
        upstream = grad_ref[q_block, :, :head]
        total = jnp.zeros((TILE, head), F32)
        for k_block in range(max(0, q_block - reach), q_block + 1):
            k_rows = slice(k_block * TILE, (k_block + 1) * TILE)
            key_half = feature_ref[k_rows, 2 * head :]
            half = dot_nt(key_ref[k_rows, :], query) * (0.5 * scale) + bias_ref[q_block - k_block]
            lean = jnp.tanh(half)
            rise = 1.0 + lean
            weight = (half * rise).astype(BF16)
            grad_weight = dot_nt(feature_ref[k_rows, :head], upstream)
            grad_score = (grad_weight * (rise * (1.0 + half * (1.0 - lean)))).astype(BF16)
            value_term = dot_nn(weight, upstream)
            key_term = dot_nn(grad_score, query_half)
            if q_block == k_block:
                value_sum[k_rows, :] = value_term
                key_sum[k_rows, :] = key_term
            else:
                value_sum[k_rows, :] += value_term
                key_sum[k_rows, :] += key_term
            total = total + dot_tn(grad_score, key_half)
        slope = slope_ref[rows, head : 2 * head].astype(F32)
        out_ref[q_block, :, head : 2 * head] = (total * (0.5 * scale) * slope).astype(BF16)
        done = [q_block - reach] if q_block < count - 1 else range(q_block - reach, count)
        for block in done:
            if block < 0:
                continue
            rows = slice(block * TILE, (block + 1) * TILE)
            value_slope = slope_ref[rows, :head].astype(F32)
            key_slope = slope_ref[rows, 2 * head :].astype(F32)
            out_ref[block, :, :head] = (value_sum[rows, :] * value_slope).astype(BF16)
            key_grad = key_sum[rows, :] * (0.5 * scale) * key_slope
            out_ref[block, :, 2 * head :] = key_grad.astype(BF16)
            if block == count // 2 - 1:
                out.send(0)


def weight_kernel(start_smem, *refs):
    mix, grad = refs[:2]
    pieces = refs[2 : PIECES + 2]
    mine_out, other_out, right_ref = refs[PIECES + 2 :]
    core = start_smem[PIECES]
    cell = TILE // 4
    mix_ref, grad_ref = mix.near, grad.near
    head = grad_ref.shape[2] // 3
    for block in range(grad_ref.shape[0]):
        rows = slice(block * TILE, (block + 1) * TILE)
        mix.wait(block)
        grad.wait(block)
        right_ref[rows, :head] = mix_ref[block, :, head:]
        right_ref[rows, head:] = grad_ref[block]
    for chunk in range(pieces[0].near.shape[1] // TILE):
        columns = slice(chunk * TILE, (chunk + 1) * TILE)
        total = jnp.zeros((TILE, 4 * head), F32)
        for index, piece in enumerate(pieces):
            ref = piece.ready()
            rows = pl.ds(pl.multiple_of(start_smem[index], HALF), ref.shape[0])
            total = total + dot_tn(ref[:, columns], right_ref[rows, :])
        for out, cells in zip((mine_out, other_out), split_cells(core, total, cell)):
            for index, part in enumerate(cells):
                out.ref[2 * chunk + index] = part.astype(BF16)
            out.send(chunk)


def input_kernel(gate_grad, grad_in, weight, token, up, out, all_grad, total):
    grad_ref = grad_in.ready()
    heads = grad_ref.shape[0]
    head = grad_ref.shape[2] // 3
    width = heads * head
    all_grad[:, :width] = gate_grad.ready()[...]
    for index in range(heads):
        for part in range(3):
            start = (part + 1) * width + index * head
            all_grad[:, start : start + head] = grad_ref[index, :, part * head : (part + 1) * head]
    for step in range(width // TILE):
        part = slice(step * TILE, (step + 1) * TILE)
        weight.wait(step)
        total[:, part] = dot_nt(all_grad[...], weight.near[part, :])
    grad = total[...]
    normed, inverse = layer_norm(token.ready()[...].astype(F32))
    first = jnp.mean(grad, axis=-1, keepdims=True)
    second = jnp.mean(grad * normed, axis=-1, keepdims=True)
    back = (grad - first - normed * second) * inverse
    out.ref[...] = (up.ready()[...].astype(F32) + back).astype(BF16)


def shift(values, by):
    return lax.ppermute(values, "seq", [(index, (index + by) % 8) for index in range(8)])


def swap(values, axis, bits, size):
    return lax.ppermute(values, axis, [(index, index ^ bits) for index in range(size)])


def gather_first(own):
    return swap(own, "seq", 1, 8), shift(own, -2), shift(own, 2)


def gather_rest(own, mate, after, before):
    half = own.shape[0] // 2
    across_low = shift(after[:half], -2)
    across_high = shift(before[half:], 2)
    mate_before = swap(before, "seq", 1, 8)
    mate_after = shift(mate, -2)
    mate_across_low = swap(across_low, "seq", 1, 8)
    mate_across_high = shift(mate_before[half:], 2)
    me = lax.axis_index("seq").astype(jnp.int32)
    other = me ^ 1
    pieces = [
        (own, me, 0),
        (mate, other, 0),
        (after, me + 2, 0),
        (before, me + 6, 0),
        (across_low, me + 4, 0),
        (across_high, me + 4, half),
        (mate_before, other + 6, 0),
        (mate_after, other + 2, 0),
        (mate_across_low, other + 4, 0),
        (mate_across_high, other + 4, half),
    ]
    starts = [(place % 8) * own.shape[0] + first for _, place, first in pieces]
    return [piece for piece, _, _ in pieces], starts


PIECES = 10
HALF = TILE // 2


def join_cores(mine, other):
    return (mine.astype(F32) + swap(other, "dp", 1, 16).astype(F32)).astype(BF16)


def send_chips(chip):
    pair = lax.axis_index("dp") // 2
    parts = [lax.dynamic_index_in_dim(chip, pair, 0, False)]
    for bits in range(1, 8):
        piece = lax.dynamic_index_in_dim(chip, pair ^ bits, 0, False)
        parts.append(swap(piece, "dp", 2 * bits, 16))
    return parts


def add_up(parts):
    total = parts[0].astype(F32)
    for part in parts[1:]:
        total = total + part.astype(F32)
    return total


def exchange(values):
    return lax.all_to_all(values, "seq", 0, 0)


def per_device(tokens, proj_weight, out_weight, rel_bias, segment_ids, distance_bucket, out_grad):
    heads, buckets = rel_bias.shape
    rows, width = tokens.shape[1:]
    head = width // heads
    length = segment_ids.shape[1]
    scale = head ** (-0.5)
    reach = 1024 // TILE
    me = lax.axis_index("seq").astype(jnp.int32)
    core = (lax.axis_index("dp") % 2).astype(jnp.int32)
    token_row = tokens[0]
    upstream = out_grad[0]

    half = call(
        norm_kernel, [shape((rows, width), BF16)], "norm"
    )(token_row)[0]
    near = gather_first(half)

    gg, gate_proj, weight = call(
        prepare_kernel,
        [shape((rows, width), F32), shape((rows, width), F32), shape((width, 3 * head), BF16)],
        "prepare",
        smem=1,
        far=(4,),
        scratch=[pltpu.VMEM((width, width), BF16), pltpu.SemaphoreType.DMA((4,))],
        flops=4 * rows * width * width,
    )(me[None], upstream, half, out_weight, proj_weight)
    one_hot = (
        distance_bucket[None, : reach * TILE] == jnp.arange(buckets, dtype=jnp.int32)[:, None]
    ).astype(F32)
    table = jnp.dot(
        lax.dynamic_slice_in_dim(rel_bias, me, 1, 0),
        one_hot,
        precision=lax.Precision.HIGHEST,
        preferred_element_type=F32,
    )
    mask = (segment_ids[0][:, None] == jnp.arange(128, dtype=jnp.int32)[None, :]).astype(BF16)
    near, gg, gate_proj, weight, table, mask = lax.optimization_barrier(
        (near, gg, gate_proj, weight, table, mask)
    )
    pieces, starts = gather_rest(half, *near)

    tiles = pltpu.VMEM((reach + 1, TILE, TILE), F32)
    features, slopes, attended = call(
        functools.partial(forward_kernel, scale),
        [
            shape((length, 3 * head), BF16),
            shape((length, 3 * head), BF16),
            shape((8, rows + 16, head), BF16),
        ],
        "forward",
        smem=1,
        out_parts={2: 8},
        scratch=[tiles, pltpu.VMEM((length, 2 * head), BF16)],
        flops=2 * length * width * 4 * head,
    )(jnp.stack(starts), weight, table, mask, *pieces)
    attended_own = exchange(attended)

    cells = shape((8, width // 16, width), BF16)
    row_shape = shape((rows, width), BF16)
    send, gate_grad, out_mine, out_other, layer_row = call(
        mix_kernel,
        [shape((heads, rows, 2 * head), BF16), row_shape, cells, cells, row_shape],
        "mix",
        smem=1,
        scratch=[pltpu.VMEM((rows, width), BF16)],
        flops=4 * rows * width * width,
    )(core[None], attended_own, gate_proj, gg, upstream, out_weight, token_row)
    mix_head = exchange(send)
    out_seq = exchange(join_cores(out_mine, out_other))
    out_cells = jnp.sum(out_seq.astype(F32), axis=0).astype(BF16).reshape(8, 16, width // 2)

    grads = call(
        functools.partial(backward_kernel, scale),
        [shape((8, rows, 3 * head), BF16)],
        "backward",
        out_parts={0: 2},
        scratch=[
            pltpu.VMEM((length, head), F32),
            pltpu.VMEM((length, head), F32),
            tiles,
            pltpu.VMEM((length, 2 * head), BF16),
        ],
        flops=10 * length * 4096 * head,
    )(table, mask, features, mix_head, slopes)[0]
    ordered, out_cells = lax.optimization_barrier((grads, out_cells))
    grads_own = exchange(ordered)

    cells = shape((8, width // 16, 4 * head), BF16)
    proj_mine, proj_other = call(
        weight_kernel,
        [cells, cells],
        "weight",
        smem=1,
        scratch=[pltpu.VMEM((length, 4 * head), BF16)],
        flops=2 * length * width * 4 * head,
    )(jnp.stack(starts + [core]), mix_head, grads, *pieces)
    parts = send_chips(
        jnp.concatenate([join_cores(proj_mine, proj_other), out_cells], axis=1)
    )
    grad_row = call(
        input_kernel,
        [shape((rows, width), BF16)],
        "input_grad",
        parts={2: width // TILE},
        scratch=[pltpu.VMEM((rows, 4 * width), BF16), pltpu.VMEM((rows, width), F32)],
        flops=8 * rows * width * width,
    )(gate_grad, grads_own, proj_weight, token_row, upstream)[0]
    grad_row, parts = lax.optimization_barrier((grad_row, parts))
    reduced = add_up(parts)
    high = width // 16
    out_out = reduced[high:].reshape(-1, width)

    final = exchange(reduced[:high].reshape(8, high // 8, 4 * head))
    few = final.shape[1]
    proj_out = final.reshape(8, few, 4, head).transpose(1, 2, 0, 3).reshape(few, 4 * width)
    return layer_row[None], grad_row[None], proj_out, out_out


def solution(mesh):
    return jax.shard_map(
        per_device,
        mesh=mesh,
        in_specs=(P("dp", "seq", None), P(), P(), P(), P("dp", None), P(), P("dp", "seq", None)),
        out_specs=(
            P("dp", "seq", None),
            P("dp", "seq", None),
            P(("dp", "seq"), None),
            P(("dp", "seq"), None),
        ),
        check_vma=False,
    )
```

```python
import functools
import jax
import jax.numpy as jnp
from jax import lax
from jax.experimental import pallas as pl
from jax.experimental.pallas import tpu as pltpu
from jax.sharding import PartitionSpec as P

EPS = 1e-05
TILE = 256
DEAD = -1e30
F32 = jnp.float32
BF16 = jnp.bfloat16


def layer_norm(values):
    average = jnp.mean(values, axis=-1, keepdims=True)
    centered = values - average
    inverse = lax.rsqrt(jnp.mean(centered * centered, axis=-1, keepdims=True) + EPS)
    return centered * inverse, inverse


def dot_nn(left, right):
    return lax.dot_general(left, right, (((1,), (0,)), ((), ())), preferred_element_type=F32)


def dot_nt(left, right):
    return lax.dot_general(left, right, (((1,), (1,)), ((), ())), preferred_element_type=F32)


def dot_tn(left, right):
    return lax.dot_general(left, right, (((0,), (0,)), ((), ())), preferred_element_type=F32)


class Incoming:
    def __init__(self, far, near, sems, first, parts):
        self.near = near
        self.size = near.shape[0] // parts
        self.copies = []
        for part in range(parts):
            rows = pl.ds(part * self.size, self.size)
            self.copies.append(
                pltpu.make_async_copy(far.at[rows], near.at[rows], sems.at[first + part])
            )
        self.pending = [True] * parts

    def start(self, part):
        if part < len(self.copies):
            self.copies[part].start()

    def wait(self, part):
        if part < len(self.copies) and self.pending[part]:
            self.copies[part].wait()
            self.pending[part] = False

    def ready(self):
        for part in range(len(self.copies)):
            self.wait(part)
        return self.near


class Outgoing:
    def __init__(self, near, far, sems, first, parts):
        self.ref = near
        size = near.shape[0] // parts
        self.copies = []
        for part in range(parts):
            rows = pl.ds(part * size, size)
            self.copies.append(
                pltpu.make_async_copy(near.at[rows], far.at[rows], sems.at[first + part])
            )
        self.sent = [False] * parts

    def send(self, part=None):
        if part is not None and len(self.copies) == 1:
            return
        for index, copy in enumerate(self.copies):
            if part in (None, index) and not self.sent[index]:
                copy.start()
                self.sent[index] = True

    def finish(self):
        for copy in self.copies:
            copy.wait()


def call(body, outs, name, smem=0, scratch=(), flops=0, far=(), parts=None, out_parts=None, limit=58, light=False):
    parts = parts or {}
    out_parts = out_parts or {}

    def run(*args):
        size = sum(a.size * a.dtype.itemsize for a in args)
        size += sum(o.size * o.dtype.itemsize for o in outs)
        near_in = [i for i in range(smem, len(args)) if i not in far]
        counts = [parts.get(i, 1) for i in near_in]
        kept = [pltpu.VMEM(args[i].shape, args[i].dtype) for i in near_in]
        kept += [pltpu.VMEM(out.shape, out.dtype) for out in outs]
        out_counts = [out_parts.get(i, 1) for i in range(len(outs))]
        kept += [pltpu.SemaphoreType.DMA((sum(counts),)), pltpu.SemaphoreType.DMA((sum(out_counts),))]

        def kernel(*refs):
            ins, refs = refs[: len(args)], refs[len(args) :]
            far_outs, refs = refs[: len(outs)], refs[len(outs) :]
            near, refs = refs[: len(near_in)], refs[len(near_in) :]
            near_outs, refs = refs[: len(outs)], refs[len(outs) :]
            in_sems, out_sems, extra = refs[0], refs[1], refs[2:]
            values = list(ins)
            first = 0
            for place, ref, count in zip(near_in, near, counts):
                values[place] = Incoming(ins[place], ref, in_sems, first, count)
                first += count
            for part in range(max(counts)):
                for place in near_in:
                    values[place].start(part)
            results = []
            first = 0
            for ref, away, count in zip(near_outs, far_outs, out_counts):
                results.append(Outgoing(ref, away, out_sems, first, count))
                first += count
            body(*values, *results, *extra)
            for place in near_in:
                values[place].ready()
            for result in results:
                result.send()
            for result in results:
                result.finish()

        return pl.pallas_call(
            kernel,
            out_shape=outs,
            in_specs=[pl.BlockSpec(memory_space=pltpu.SMEM)] * smem
            + [pl.BlockSpec(memory_space=pltpu.HBM)] * (len(args) - smem),
            out_specs=[pl.BlockSpec(memory_space=pltpu.HBM)] * len(outs),
            scratch_shapes=kept + list(scratch),
            compiler_params=pltpu.CompilerParams(vmem_limit_bytes=limit * 1024 * 1024),
            cost_estimate=pl.CostEstimate(flops=flops, bytes_accessed=0 if light else size, transcendentals=0),
            name=name,
        )(*args)

    return run


def shape(dims, kind):
    return jax.ShapeDtypeStruct(dims, kind)


def norm_kernel(token, half):
    for part in range(len(token.copies)):
        token.wait(part)
        rows = slice(part * token.size, (part + 1) * token.size)
        normed, _ = layer_norm(token.near[rows, :].astype(F32))
        half.ref[rows, :] = normed.astype(BF16)
        half.send(part)


def prepare_kernel(me_smem, up, half, out_w, weight_far, gg, gate, weight, gate_w, sems):
    width = gate_w.shape[0]
    head = weight.ref.shape[1] // 3
    copies = [pltpu.make_async_copy(weight_far.at[:, :width], gate_w, sems.at[0])]
    for part in range(3):
        start = pl.multiple_of((part + 1) * width + me_smem[0] * head, head)
        source = weight_far.at[:, pl.ds(start, head)]
        target = weight.ref.at[:, part * head : (part + 1) * head]
        copies.append(pltpu.make_async_copy(source, target, sems.at[part + 1]))
    for copy in copies:
        copy.start()
    gg.ref[...] = dot_nt(up.ready()[...], out_w.ready()[...])
    gg.send()
    copies[0].wait()
    gate.ref[...] = dot_nn(half.ready()[...], gate_w[...])
    gate.send()
    for copy in copies[1:]:
        copy.wait()


def bias_tiles(table_ref, tile_ref, turned):
    count = tile_ref.shape[0]
    key_at = lax.broadcasted_iota(jnp.int32, (TILE, TILE), 0)
    query_at = lax.broadcasted_iota(jnp.int32, (TILE, TILE), 1)
    for step in range(count):
        if step < count - 1:
            later = table_ref[:, step * TILE : (step + 1) * TILE]
        else:
            later = jnp.zeros((1, TILE), F32)
        if step > 0:
            earlier = table_ref[:, (step - 1) * TILE : step * TILE]
        else:
            earlier = jnp.zeros((1, TILE), F32)
        window = jnp.broadcast_to(jnp.concatenate([later, earlier], axis=1), (TILE, 2 * TILE))
        rolled = 0.5 * pltpu.roll(window, 0, 1, stride=1, stride_axis=0)[:, :TILE]
        if step == 0:
            rolled = jnp.where(key_at <= query_at, rolled, DEAD)
        tile_ref[step] = rolled if turned else rolled.T


def key_mask(mask):
    return ((1.0 - mask.astype(F32)) * DEAD).astype(BF16)


def forward_kernel(scale, start_smem, *refs):
    weight, table, mask = refs[:3]
    pieces = refs[3 : PIECES + 3]
    feature, slope, attended, bias_ref, key_ref = refs[PIECES + 3 :]
    feature_ref, slope_ref = feature.ref, slope.ref
    count, _, head = attended.ref.shape
    reach = bias_ref.shape[0] - 1
    row_at = lax.broadcasted_iota(jnp.int32, (16, HALF), 0)
    bias_tiles(table.ready(), bias_ref, False)
    mask_ref = mask.ready()
    key_ref[:, head:] = key_mask(mask_ref[...])
    weight_ref = weight.ready()
    for index, piece in enumerate(pieces):
        ref = piece.ready()
        rows = pl.ds(pl.multiple_of(start_smem[index], HALF), ref.shape[0])
        half = 0.5 * dot_nn(ref[...], weight_ref[...])
        lean = jnp.tanh(half)
        rise = 1.0 + lean
        made = (half * rise).astype(BF16)
        feature_ref[rows, :] = made
        key_ref[rows, :head] = made[:, 2 * head :]
        slope_ref[rows, :] = (0.5 * rise * (1.0 + half * (1.0 - lean))).astype(BF16)
    feature.send()
    slope.send()
    for q_block in range(count):
        rows = slice(q_block * TILE, (q_block + 1) * TILE)
        query = jnp.concatenate([feature_ref[rows, head : 2 * head], mask_ref[rows, :]], axis=1)
        total = jnp.zeros((TILE, head), F32)
        for k_block in range(max(0, q_block - reach), q_block + 1):
            k_rows = slice(k_block * TILE, (k_block + 1) * TILE)
            half = dot_nt(query, key_ref[k_rows, :]) * (0.5 * scale) + bias_ref[q_block - k_block]
            weights = half * (1.0 + jnp.tanh(half))
            total = total + dot_nn(weights.astype(BF16), feature_ref[k_rows, :head])
        average = jnp.mean(total, axis=1, keepdims=True)
        attended.ref[q_block, :TILE, :] = (total - average).astype(BF16)
        wide = jnp.broadcast_to(average, total.shape).T[:16, :]
        high = wide.astype(BF16).astype(F32)
        low = wide - high
        packed = jnp.where(row_at == 0, high[:, :HALF], high[:, HALF:])
        packed = jnp.where(row_at == 2, low[:, :HALF], packed)
        packed = jnp.where(row_at == 3, low[:, HALF:], packed)
        attended.ref[q_block, TILE:, :] = packed.astype(BF16)
        attended.send(q_block)


def split_cells(core, total, cell):
    low = [total[2 * k * cell : (2 * k + 1) * cell] for k in range(2)]
    high = [total[(2 * k + 1) * cell : (2 * k + 2) * cell] for k in range(2)]
    mine = [jnp.where(core == 0, x, y) for x, y in zip(low, high)]
    other = [jnp.where(core == 0, y, x) for x, y in zip(low, high)]
    return mine, other


def mix_kernel(
    attended_in, gate_in, gg_in, send_out, gate_grad_out, gated_out
):
    attended_ref = attended_in.ready()
    send_ref = send_out.ref
    heads, _, head = attended_ref.shape
    rows = []
    for index in range(heads):
        packed = attended_ref[index, TILE:, :].astype(F32)
        rows.append(
            jnp.concatenate([packed[0:1] + packed[2:3], packed[1:2] + packed[3:4]], axis=1)
        )
    averages = jnp.concatenate(rows, axis=0).T
    attended = jnp.concatenate(
        [
            attended_ref[index, :TILE, :].astype(F32) + averages[:, index : index + 1]
            for index in range(heads)
        ],
        axis=1,
    )
    mixed, inverse = layer_norm(attended)
    half = 0.5 * gate_in.ready()[...]
    lean = jnp.tanh(half)
    rise = 1.0 + lean
    gate = (half * rise).astype(BF16).astype(F32)
    gg = gg_in.ready()[...]
    gated_out.ref[...] = (mixed * gate).astype(BF16)
    gate_grad = (gg * mixed * (0.5 * rise * (1.0 + half * (1.0 - lean)))).astype(BF16)
    gate_grad_out.ref[...] = gate_grad
    gate_grad_out.send()
    grad = gg * gate
    first = jnp.mean(grad, axis=-1, keepdims=True)
    second = jnp.mean(grad * mixed, axis=-1, keepdims=True)
    grad = ((grad - first - mixed * second) * inverse).astype(BF16)
    for index in range(heads):
        columns = slice(index * head, (index + 1) * head)
        send_ref[index, :, :head] = grad[:, columns]
        send_ref[index, :, head:] = gate_grad[:, columns]


def backward_kernel(
    scale, table, mask, feature, grad_in, slope_in, out, key_sum, value_sum, bias_ref, key_ref
):
    head = key_sum.shape[1]
    out_ref = out.ref
    bias_tiles(table.ready(), bias_ref, True)
    mask_ref, feature_ref = mask.near, feature.near
    grad_ref, slope_ref = grad_in.near, slope_in.near
    count = grad_ref.shape[0]
    reach = bias_ref.shape[0] - 1
    for q_block in range(count):
        rows = slice(q_block * TILE, (q_block + 1) * TILE)
        if q_block % 2 == 0:
            for source in (mask, feature, grad_in):
                source.wait(q_block // 2)
        key_ref[rows, :head] = feature_ref[rows, 2 * head :]
        key_ref[rows, head:] = key_mask(mask_ref[rows, :])
        query_half = feature_ref[rows, head : 2 * head]
        query = jnp.concatenate([query_half, mask_ref[rows, :]], axis=1)
        upstream = grad_ref[q_block, :, :head]
        total = jnp.zeros((TILE, head), F32)
        for k_block in range(max(0, q_block - reach), q_block + 1):
            k_rows = slice(k_block * TILE, (k_block + 1) * TILE)
            key_half = feature_ref[k_rows, 2 * head :]
            half = dot_nt(key_ref[k_rows, :], query) * (0.5 * scale) + bias_ref[q_block - k_block]
            lean = jnp.tanh(half)
            rise = 1.0 + lean
            weight = (half * rise).astype(BF16)
            grad_weight = dot_nt(feature_ref[k_rows, :head], upstream)
            grad_score = (grad_weight * (rise * (1.0 + half * (1.0 - lean)))).astype(BF16)
            value_term = dot_nn(weight, upstream)
            key_term = dot_nn(grad_score, query_half)
            if q_block == k_block:
                value_sum[k_rows, :] = value_term
                key_sum[k_rows, :] = key_term
            else:
                value_sum[k_rows, :] += value_term
                key_sum[k_rows, :] += key_term
            total = total + dot_tn(grad_score, key_half)
        slope_in.wait(q_block)
        slope = slope_ref[rows, head : 2 * head].astype(F32)
        out_ref[q_block, :, head : 2 * head] = (total * (0.5 * scale) * slope).astype(BF16)
        done = [q_block - reach] if q_block < count - 1 else range(q_block - reach, count)
        for block in done:
            if block < 0:
                continue
            rows = slice(block * TILE, (block + 1) * TILE)
            value_slope = slope_ref[rows, :head].astype(F32)
            key_slope = slope_ref[rows, 2 * head :].astype(F32)
            out_ref[block, :, :head] = (value_sum[rows, :] * value_slope).astype(BF16)
            key_grad = key_sum[rows, :] * (0.5 * scale) * key_slope
            out_ref[block, :, 2 * head :] = key_grad.astype(BF16)
            if block == count // 2 - 1:
                out.send(0)


def sums_kernel(info_smem, *refs):
    mix, grad = refs[:2]
    pieces = refs[2 : PIECES + 2]
    gated, up, out_w, token, mine_out = refs[PIECES + 2 : PIECES + 7]
    others, layer, right_ref = refs[PIECES + 7 : -2], refs[-2], refs[-1]
    core = info_smem[PIECES]
    cell = TILE // 4
    mix_ref, grad_ref = mix.ready(), grad.ready()
    head = grad_ref.shape[2] // 3
    for block in range(grad_ref.shape[0]):
        rows = slice(block * TILE, (block + 1) * TILE)
        right_ref[rows, :head] = mix_ref[block, :, head:]
        right_ref[rows, head:] = grad_ref[block]
    for chunk in range(pieces[0].near.shape[1] // TILE):
        columns = slice(chunk * TILE, (chunk + 1) * TILE)
        total = jnp.zeros((TILE, 4 * head), F32)
        for index, piece in enumerate(pieces):
            ref = piece.ready()
            rows = pl.ds(pl.multiple_of(info_smem[index], HALF), ref.shape[0])
            total = total + dot_tn(ref[:, columns], right_ref[rows, :])
        mine, other = split_cells(core, total, cell)
        for index in range(2):
            mine_out.ref[2 * chunk + index, :, : 4 * head] = mine[index].astype(BF16)
            others[0].ref[2 * chunk + index] = other[index].astype(BF16)
    others[0].send()
    gated_ref = gated.ready()
    up_rows = up.ready()[...]
    for chunk in range(gated_ref.shape[1] // TILE):
        total = dot_tn(gated_ref[:, chunk * TILE : (chunk + 1) * TILE], up_rows)
        mine, other = split_cells(core, total, cell)
        for index in range(2):
            mine_out.ref[2 * chunk + index, :, 4 * head :] = mine[index].astype(BF16)
            for out, first in zip(others[1:], (0, 4 * head)):
                columns = slice(first, first + 4 * head)
                out.ref[2 * chunk + index] = other[index][:, columns].astype(BF16)
    mine_out.send()
    for out in others[1:]:
        out.send()
    result = dot_nn(gated_ref[...], out_w.ready()[...])
    layer.ref[...] = (token.ready()[...].astype(F32) + result).astype(BF16)


def join_kernel(mine, *refs):
    others, out = refs[:-1], refs[-1]
    mine_ref = mine.ready()
    first = 0
    for other in others:
        ref = other.ready()
        columns = slice(first, first + ref.shape[2])
        total = mine_ref[:, :, columns].astype(F32) + ref[...].astype(F32)
        out.ref[:, :, columns] = total.astype(BF16)
        first += ref.shape[2]


def input_kernel(gate_grad, grad_in, weight, token, up, out, all_grad, total):
    grad_ref = grad_in.ready()
    heads = grad_ref.shape[0]
    head = grad_ref.shape[2] // 3
    width = heads * head
    all_grad[:, :width] = gate_grad.ready()[...]
    for index in range(heads):
        for part in range(3):
            start = (part + 1) * width + index * head
            all_grad[:, start : start + head] = grad_ref[index, :, part * head : (part + 1) * head]
    for step in range(width // TILE):
        part = slice(step * TILE, (step + 1) * TILE)
        weight.wait(step)
        total[:, part] = dot_nt(all_grad[...], weight.near[part, :])
    grad = total[...]
    normed, inverse = layer_norm(token.ready()[...].astype(F32))
    first = jnp.mean(grad, axis=-1, keepdims=True)
    second = jnp.mean(grad * normed, axis=-1, keepdims=True)
    back = (grad - first - normed * second) * inverse
    out.ref[...] = (up.ready()[...].astype(F32) + back).astype(BF16)


def shift(values, by):
    return lax.ppermute(values, "seq", [(index, (index + by) % 8) for index in range(8)])


def swap(values, axis, bits, size):
    return lax.ppermute(values, axis, [(index, index ^ bits) for index in range(size)])


def gather_first(own):
    return swap(own, "seq", 1, 8), shift(own, -2), shift(own, 2)


def gather_rest(own, mate, after, before):
    half = own.shape[0] // 2
    across_low = shift(after[:half], -2)
    across_high = shift(before[half:], 2)
    mate_before = swap(before, "seq", 1, 8)
    mate_after = shift(mate, -2)
    mate_across_low = swap(across_low, "seq", 1, 8)
    mate_across_high = shift(mate_before[half:], 2)
    me = lax.axis_index("seq").astype(jnp.int32)
    other = me ^ 1
    pieces = [
        (own, me, 0),
        (mate, other, 0),
        (after, me + 2, 0),
        (before, me + 6, 0),
        (across_low, me + 4, 0),
        (across_high, me + 4, half),
        (mate_before, other + 6, 0),
        (mate_after, other + 2, 0),
        (mate_across_low, other + 4, 0),
        (mate_across_high, other + 4, half),
    ]
    starts = [(place % 8) * own.shape[0] + first for _, place, first in pieces]
    return [piece for piece, _, _ in pieces], starts


PIECES = 10
HALF = TILE // 2


CHIPS = [
    [place * 8 + part for place in range(core, 16, 2) for part in range(8)] for core in range(2)
]


def exchange_chips(values):
    return lax.all_to_all(values, ("dp", "seq"), 0, 0, axis_index_groups=CHIPS)


def exchange(values):
    return lax.all_to_all(values, "seq", 0, 0)


def per_device(tokens, proj_weight, out_weight, rel_bias, segment_ids, distance_bucket, out_grad):
    heads, buckets = rel_bias.shape
    rows, width = tokens.shape[1:]
    head = width // heads
    length = segment_ids.shape[1]
    scale = head ** (-0.5)
    reach = 1024 // TILE
    me = lax.axis_index("seq").astype(jnp.int32)
    core = (lax.axis_index("dp") % 2).astype(jnp.int32)
    token_row = tokens[0]
    upstream = out_grad[0]

    half = call(
        norm_kernel, [shape((rows, width), BF16)], "norm"
    )(token_row)[0]
    near = gather_first(half)

    gg, gate_proj, weight = call(
        prepare_kernel,
        [shape((rows, width), F32), shape((rows, width), F32), shape((width, 3 * head), BF16)],
        "prepare",
        smem=1,
        far=(4,),
        scratch=[pltpu.VMEM((width, width), BF16), pltpu.SemaphoreType.DMA((4,))],
        flops=4 * rows * width * width,
    )(me[None], upstream, half, out_weight, proj_weight)
    one_hot = (
        distance_bucket[None, : reach * TILE] == jnp.arange(buckets, dtype=jnp.int32)[:, None]
    ).astype(F32)
    table = jnp.dot(
        lax.dynamic_slice_in_dim(rel_bias, me, 1, 0),
        one_hot,
        precision=lax.Precision.HIGHEST,
        preferred_element_type=F32,
    )
    mask = (segment_ids[0][:, None] == jnp.arange(128, dtype=jnp.int32)[None, :]).astype(BF16)
    near, gg, gate_proj, weight, table, mask = lax.optimization_barrier(
        (near, gg, gate_proj, weight, table, mask)
    )
    pieces, starts = gather_rest(half, *near)
    info = lax.optimization_barrier(jnp.stack(starts + [core]))

    tiles = pltpu.VMEM((reach + 1, TILE, TILE), F32)
    features, slopes, attended = call(
        functools.partial(forward_kernel, scale),
        [
            shape((length, 3 * head), BF16),
            shape((length, 3 * head), BF16),
            shape((8, rows + 16, head), BF16),
        ],
        "forward",
        smem=1,
        out_parts={2: 8},
        scratch=[tiles, pltpu.VMEM((length, 2 * head), BF16)],
        flops=2 * length * width * 4 * head,
    )(info, weight, table, mask, *pieces)
    attended_own = exchange(attended)

    row_shape = shape((rows, width), BF16)
    send, gate_grad, gated = call(
        mix_kernel,
        [shape((heads, rows, 2 * head), BF16), row_shape, row_shape],
        "mix",
    )(attended_own, gate_proj, gg)
    mix_head = exchange(send)

    grads = call(
        functools.partial(backward_kernel, scale),
        [shape((8, rows, 3 * head), BF16)],
        "backward",
        parts={1: 4, 2: 4, 3: 4},
        out_parts={0: 2},
        scratch=[
            pltpu.VMEM((length, head), F32),
            pltpu.VMEM((length, head), F32),
            tiles,
            pltpu.VMEM((length, 2 * head), BF16),
        ],
        flops=10 * length * 4096 * head,
    )(table, mask, features, mix_head, slopes)[0]
    grads_own = exchange(grads)

    cells = shape((8, width // 16, 4 * head + width), BF16)
    third = shape((8, width // 16, 4 * head), BF16)
    mine, first, second, last, layer_row = call(
        sums_kernel,
        [cells, third, third, third, row_shape],
        "sums",
        smem=1,
        scratch=[pltpu.VMEM((length, 4 * head), BF16)],
        flops=2 * length * width * 4 * head + 4 * rows * width * width,
    )(info, mix_head, grads, *pieces, gated, upstream, out_weight, token_row)
    others = [swap(part, "dp", 1, 16) for part in (first, second, last)]
    both = call(join_kernel, [cells], "join", light=True)(mine, *others)[0]
    both, grads_own = lax.optimization_barrier((both, grads_own))
    few = width // 128
    parts = exchange_chips(both.reshape(64, few, 4 * head + width))
    final = jnp.sum(parts.reshape(8, 8, few, -1).astype(F32), axis=0)
    proj_out = final[:, :, : 4 * head].reshape(8, few, 4, head)
    proj_out = proj_out.transpose(1, 2, 0, 3).reshape(few, 4 * width)
    out_out = jnp.sum(final[:, :, 4 * head :], axis=0)

    grad_row = call(
        input_kernel,
        [shape((rows, width), BF16)],
        "input_grad",
        parts={2: width // TILE},
        scratch=[pltpu.VMEM((rows, 4 * width), BF16), pltpu.VMEM((rows, width), F32)],
        flops=8 * rows * width * width,
    )(gate_grad, grads_own, proj_weight, token_row, upstream)[0]
    return layer_row[None], grad_row[None], proj_out, out_out


def solution(mesh):
    return jax.shard_map(
        per_device,
        mesh=mesh,
        in_specs=(P("dp", "seq", None), P(), P(), P(), P("dp", None), P(), P("dp", "seq", None)),
        out_specs=(
            P("dp", "seq", None),
            P("dp", "seq", None),
            P(("dp", "seq"), None),
            P(("dp", "seq"), None),
        ),
        check_vma=False,
    )
```

```python
import functools
import jax
import jax.numpy as jnp
from jax import lax
from jax.experimental import pallas as pl
from jax.experimental.pallas import tpu as pltpu
from jax.sharding import PartitionSpec as P

EPS = 1e-05
TILE = 256
DEAD = -1e30
F32 = jnp.float32
BF16 = jnp.bfloat16


def layer_norm(values):
    average = jnp.mean(values, axis=-1, keepdims=True)
    centered = values - average
    inverse = lax.rsqrt(jnp.mean(centered * centered, axis=-1, keepdims=True) + EPS)
    return centered * inverse, inverse


def dot_nn(left, right):
    return lax.dot_general(left, right, (((1,), (0,)), ((), ())), preferred_element_type=F32)


def dot_nt(left, right):
    return lax.dot_general(left, right, (((1,), (1,)), ((), ())), preferred_element_type=F32)


def dot_tn(left, right):
    return lax.dot_general(left, right, (((0,), (0,)), ((), ())), preferred_element_type=F32)


class Incoming:
    def __init__(self, far, near, sems, first, parts):
        self.near = near
        self.size = near.shape[0] // parts
        self.copies = []
        for part in range(parts):
            rows = pl.ds(part * self.size, self.size)
            self.copies.append(
                pltpu.make_async_copy(far.at[rows], near.at[rows], sems.at[first + part])
            )
        self.pending = [True] * parts

    def start(self, part):
        if part < len(self.copies):
            self.copies[part].start()

    def wait(self, part):
        if part < len(self.copies) and self.pending[part]:
            self.copies[part].wait()
            self.pending[part] = False

    def ready(self):
        for part in range(len(self.copies)):
            self.wait(part)
        return self.near


class Outgoing:
    def __init__(self, near, far, sems, first, parts):
        self.ref = near
        size = near.shape[0] // parts
        self.copies = []
        for part in range(parts):
            rows = pl.ds(part * size, size)
            self.copies.append(
                pltpu.make_async_copy(near.at[rows], far.at[rows], sems.at[first + part])
            )
        self.sent = [False] * parts

    def send(self, part=None):
        if part is not None and len(self.copies) == 1:
            return
        for index, copy in enumerate(self.copies):
            if part in (None, index) and not self.sent[index]:
                copy.start()
                self.sent[index] = True

    def finish(self):
        for copy in self.copies:
            copy.wait()


def call(body, outs, name, smem=0, scratch=(), flops=0, far=(), parts=None, out_parts=None, limit=58, light=False):
    parts = parts or {}
    out_parts = out_parts or {}

    def run(*args):
        size = sum(a.size * a.dtype.itemsize for a in args)
        size += sum(o.size * o.dtype.itemsize for o in outs)
        near_in = [i for i in range(smem, len(args)) if i not in far]
        counts = [parts.get(i, 1) for i in near_in]
        kept = [pltpu.VMEM(args[i].shape, args[i].dtype) for i in near_in]
        kept += [pltpu.VMEM(out.shape, out.dtype) for out in outs]
        out_counts = [out_parts.get(i, 1) for i in range(len(outs))]
        kept += [pltpu.SemaphoreType.DMA((sum(counts),)), pltpu.SemaphoreType.DMA((sum(out_counts),))]

        def kernel(*refs):
            ins, refs = refs[: len(args)], refs[len(args) :]
            far_outs, refs = refs[: len(outs)], refs[len(outs) :]
            near, refs = refs[: len(near_in)], refs[len(near_in) :]
            near_outs, refs = refs[: len(outs)], refs[len(outs) :]
            in_sems, out_sems, extra = refs[0], refs[1], refs[2:]
            values = list(ins)
            first = 0
            for place, ref, count in zip(near_in, near, counts):
                values[place] = Incoming(ins[place], ref, in_sems, first, count)
                first += count
            for part in range(max(counts)):
                for place in near_in:
                    values[place].start(part)
            results = []
            first = 0
            for ref, away, count in zip(near_outs, far_outs, out_counts):
                results.append(Outgoing(ref, away, out_sems, first, count))
                first += count
            body(*values, *results, *extra)
            for place in near_in:
                values[place].ready()
            for result in results:
                result.send()
            for result in results:
                result.finish()

        return pl.pallas_call(
            kernel,
            out_shape=outs,
            in_specs=[pl.BlockSpec(memory_space=pltpu.SMEM)] * smem
            + [pl.BlockSpec(memory_space=pltpu.HBM)] * (len(args) - smem),
            out_specs=[pl.BlockSpec(memory_space=pltpu.HBM)] * len(outs),
            scratch_shapes=kept + list(scratch),
            compiler_params=pltpu.CompilerParams(vmem_limit_bytes=limit * 1024 * 1024),
            cost_estimate=pl.CostEstimate(flops=flops, bytes_accessed=0 if light else size, transcendentals=0),
            name=name,
        )(*args)

    return run


def shape(dims, kind):
    return jax.ShapeDtypeStruct(dims, kind)


def norm_kernel(token, half):
    for part in range(len(token.copies)):
        token.wait(part)
        rows = slice(part * token.size, (part + 1) * token.size)
        normed, _ = layer_norm(token.near[rows, :].astype(F32))
        half.ref[rows, :] = normed.astype(BF16)
        half.send(part)


def prepare_kernel(me_smem, up, half, out_w, weight_far, gg, gate, weight, gate_w, sems):
    width = gate_w.shape[0]
    head = weight.ref.shape[1] // 3
    copies = [pltpu.make_async_copy(weight_far.at[:, :width], gate_w, sems.at[0])]
    for part in range(3):
        start = pl.multiple_of((part + 1) * width + me_smem[0] * head, head)
        source = weight_far.at[:, pl.ds(start, head)]
        target = weight.ref.at[:, part * head : (part + 1) * head]
        copies.append(pltpu.make_async_copy(source, target, sems.at[part + 1]))
    for copy in copies:
        copy.start()
    gg.ref[...] = dot_nt(up.ready()[...], out_w.ready()[...])
    gg.send()
    copies[0].wait()
    gate.ref[...] = dot_nn(half.ready()[...], gate_w[...])
    gate.send()
    for copy in copies[1:]:
        copy.wait()


def bias_tiles(table_ref, tile_ref, turned):
    count = tile_ref.shape[0]
    key_at = lax.broadcasted_iota(jnp.int32, (TILE, TILE), 0)
    query_at = lax.broadcasted_iota(jnp.int32, (TILE, TILE), 1)
    for step in range(count):
        if step < count - 1:
            later = table_ref[:, step * TILE : (step + 1) * TILE]
        else:
            later = jnp.zeros((1, TILE), F32)
        if step > 0:
            earlier = table_ref[:, (step - 1) * TILE : step * TILE]
        else:
            earlier = jnp.zeros((1, TILE), F32)
        window = jnp.broadcast_to(jnp.concatenate([later, earlier], axis=1), (TILE, 2 * TILE))
        rolled = 0.5 * pltpu.roll(window, 0, 1, stride=1, stride_axis=0)[:, :TILE]
        if step == 0:
            rolled = jnp.where(key_at <= query_at, rolled, DEAD)
        tile_ref[step] = rolled if turned else rolled.T


def key_mask(mask):
    return ((1.0 - mask.astype(F32)) * DEAD).astype(BF16)


def forward_kernel(scale, start_smem, *refs):
    weight, table, mask = refs[:3]
    pieces = refs[3 : PIECES + 3]
    feature, slope, attended, bias_ref, key_ref = refs[PIECES + 3 :]
    feature_ref, slope_ref = feature.ref, slope.ref
    count, _, head = attended.ref.shape
    reach = bias_ref.shape[0] - 1
    row_at = lax.broadcasted_iota(jnp.int32, (16, HALF), 0)
    bias_tiles(table.ready(), bias_ref, False)
    mask_ref = mask.ready()
    key_ref[:, head:] = key_mask(mask_ref[...])
    weight_ref = weight.ready()
    for index, piece in enumerate(pieces):
        ref = piece.ready()
        rows = pl.ds(pl.multiple_of(start_smem[index], HALF), ref.shape[0])
        half = 0.5 * dot_nn(ref[...], weight_ref[...])
        lean = jnp.tanh(half)
        rise = 1.0 + lean
        made = (half * rise).astype(BF16)
        feature_ref[rows, :] = made
        key_ref[rows, :head] = made[:, 2 * head :]
        slope_ref[rows, :] = (0.5 * rise * (1.0 + half * (1.0 - lean))).astype(BF16)
    feature.send()
    slope.send()
    for q_block in range(count):
        rows = slice(q_block * TILE, (q_block + 1) * TILE)
        query = jnp.concatenate([feature_ref[rows, head : 2 * head], mask_ref[rows, :]], axis=1)
        total = jnp.zeros((TILE, head), F32)
        for k_block in range(max(0, q_block - reach), q_block + 1):
            k_rows = slice(k_block * TILE, (k_block + 1) * TILE)
            half = dot_nt(query, key_ref[k_rows, :]) * (0.5 * scale) + bias_ref[q_block - k_block]
            weights = half * (1.0 + jnp.tanh(half))
            total = total + dot_nn(weights.astype(BF16), feature_ref[k_rows, :head])
        average = jnp.mean(total, axis=1, keepdims=True)
        attended.ref[q_block, :TILE, :] = (total - average).astype(BF16)
        wide = jnp.broadcast_to(average, total.shape).T[:16, :]
        high = wide.astype(BF16).astype(F32)
        low = wide - high
        packed = jnp.where(row_at == 0, high[:, :HALF], high[:, HALF:])
        packed = jnp.where(row_at == 2, low[:, :HALF], packed)
        packed = jnp.where(row_at == 3, low[:, HALF:], packed)
        attended.ref[q_block, TILE:, :] = packed.astype(BF16)
        attended.send(q_block)


def split_cells(core, total, cell):
    low = [total[2 * k * cell : (2 * k + 1) * cell] for k in range(2)]
    high = [total[(2 * k + 1) * cell : (2 * k + 2) * cell] for k in range(2)]
    mine = [jnp.where(core == 0, x, y) for x, y in zip(low, high)]
    other = [jnp.where(core == 0, y, x) for x, y in zip(low, high)]
    return mine, other


def mix_kernel(
    attended_in, gate_in, gg_in, send_out, gate_grad_out, gated_out
):
    attended_ref = attended_in.ready()
    send_ref = send_out.ref
    heads, _, head = attended_ref.shape
    rows = []
    for index in range(heads):
        packed = attended_ref[index, TILE:, :].astype(F32)
        rows.append(
            jnp.concatenate([packed[0:1] + packed[2:3], packed[1:2] + packed[3:4]], axis=1)
        )
    averages = jnp.concatenate(rows, axis=0).T
    attended = jnp.concatenate(
        [
            attended_ref[index, :TILE, :].astype(F32) + averages[:, index : index + 1]
            for index in range(heads)
        ],
        axis=1,
    )
    mixed, inverse = layer_norm(attended)
    half = 0.5 * gate_in.ready()[...]
    lean = jnp.tanh(half)
    rise = 1.0 + lean
    gate = (half * rise).astype(BF16).astype(F32)
    gg = gg_in.ready()[...]
    gated_out.ref[...] = (mixed * gate).astype(BF16)
    gate_grad = (gg * mixed * (0.5 * rise * (1.0 + half * (1.0 - lean)))).astype(BF16)
    gate_grad_out.ref[...] = gate_grad
    gate_grad_out.send()
    grad = gg * gate
    first = jnp.mean(grad, axis=-1, keepdims=True)
    second = jnp.mean(grad * mixed, axis=-1, keepdims=True)
    grad = ((grad - first - mixed * second) * inverse).astype(BF16)
    for index in range(heads):
        columns = slice(index * head, (index + 1) * head)
        send_ref[index, :, :head] = grad[:, columns]
        send_ref[index, :, head:] = gate_grad[:, columns]


def backward_kernel(
    scale, table, mask, feature, grad_in, slope_in, out, key_sum, value_sum, bias_ref, key_ref
):
    head = key_sum.shape[1]
    out_ref = out.ref
    bias_tiles(table.ready(), bias_ref, True)
    mask_ref, feature_ref = mask.near, feature.near
    grad_ref, slope_ref = grad_in.near, slope_in.near
    count = grad_ref.shape[0]
    reach = bias_ref.shape[0] - 1
    for q_block in range(count):
        rows = slice(q_block * TILE, (q_block + 1) * TILE)
        if q_block % 2 == 0:
            for source in (mask, feature, grad_in):
                source.wait(q_block // 2)
        key_ref[rows, :head] = feature_ref[rows, 2 * head :]
        key_ref[rows, head:] = key_mask(mask_ref[rows, :])
        query_half = feature_ref[rows, head : 2 * head]
        query = jnp.concatenate([query_half, mask_ref[rows, :]], axis=1)
        upstream = grad_ref[q_block, :, :head]
        total = jnp.zeros((TILE, head), F32)
        for k_block in range(max(0, q_block - reach), q_block + 1):
            k_rows = slice(k_block * TILE, (k_block + 1) * TILE)
            key_half = feature_ref[k_rows, 2 * head :]
            half = dot_nt(key_ref[k_rows, :], query) * (0.5 * scale) + bias_ref[q_block - k_block]
            lean = jnp.tanh(half)
            rise = 1.0 + lean
            weight = (half * rise).astype(BF16)
            grad_weight = dot_nt(feature_ref[k_rows, :head], upstream)
            grad_score = (grad_weight * (rise * (1.0 + half * (1.0 - lean)))).astype(BF16)
            value_term = dot_nn(weight, upstream)
            key_term = dot_nn(grad_score, query_half)
            if q_block == k_block:
                value_sum[k_rows, :] = value_term
                key_sum[k_rows, :] = key_term
            else:
                value_sum[k_rows, :] += value_term
                key_sum[k_rows, :] += key_term
            total = total + dot_tn(grad_score, key_half)
        slope_in.wait(q_block)
        slope = slope_ref[rows, head : 2 * head].astype(F32)
        out_ref[q_block, :, head : 2 * head] = (total * (0.5 * scale) * slope).astype(BF16)
        done = [q_block - reach] if q_block < count - 1 else range(q_block - reach, count)
        for block in done:
            if block < 0:
                continue
            rows = slice(block * TILE, (block + 1) * TILE)
            value_slope = slope_ref[rows, :head].astype(F32)
            key_slope = slope_ref[rows, 2 * head :].astype(F32)
            out_ref[block, :, :head] = (value_sum[rows, :] * value_slope).astype(BF16)
            key_grad = key_sum[rows, :] * (0.5 * scale) * key_slope
            out_ref[block, :, 2 * head :] = key_grad.astype(BF16)
            if block == count // 2 - 1:
                out.send(0)


def sums_kernel(info_smem, *refs):
    mix, grad = refs[:2]
    pieces = refs[2 : PIECES + 2]
    gated, up, mine_out = refs[PIECES + 2 : PIECES + 5]
    others, right_ref = refs[PIECES + 5 : -1], refs[-1]
    core = info_smem[PIECES]
    cell = TILE // 4
    mix_ref, grad_ref = mix.ready(), grad.ready()
    head = grad_ref.shape[2] // 3
    for block in range(grad_ref.shape[0]):
        rows = slice(block * TILE, (block + 1) * TILE)
        right_ref[rows, :head] = mix_ref[block, :, head:]
        right_ref[rows, head:] = grad_ref[block]
    for chunk in range(pieces[0].near.shape[1] // TILE):
        columns = slice(chunk * TILE, (chunk + 1) * TILE)
        total = jnp.zeros((TILE, 4 * head), F32)
        for index, piece in enumerate(pieces):
            ref = piece.ready()
            rows = pl.ds(pl.multiple_of(info_smem[index], HALF), ref.shape[0])
            total = total + dot_tn(ref[:, columns], right_ref[rows, :])
        mine, other = split_cells(core, total, cell)
        for index in range(2):
            mine_out.ref[2 * chunk + index, :, : 4 * head] = mine[index].astype(BF16)
            others[0].ref[2 * chunk + index] = other[index].astype(BF16)
    others[0].send()
    gated_ref = gated.ready()
    up_rows = up.ready()[...]
    for chunk in range(gated_ref.shape[1] // TILE):
        total = dot_tn(gated_ref[:, chunk * TILE : (chunk + 1) * TILE], up_rows)
        mine, other = split_cells(core, total, cell)
        for index in range(2):
            mine_out.ref[2 * chunk + index, :, 4 * head :] = mine[index].astype(BF16)
            for out, first in zip(others[1:], (0, 4 * head)):
                columns = slice(first, first + 4 * head)
                out.ref[2 * chunk + index] = other[index][:, columns].astype(BF16)
    mine_out.send()
    for out in others[1:]:
        out.send()


def join_kernel(mine, *refs):
    others, out = refs[:-1], refs[-1]
    mine_ref = mine.ready()
    first = 0
    for other in others:
        ref = other.ready()
        columns = slice(first, first + ref.shape[2])
        total = mine_ref[:, :, columns].astype(F32) + ref[...].astype(F32)
        out.ref[:, :, columns] = total.astype(BF16)
        first += ref.shape[2]


def input_kernel(
    gate_grad, grad_in, weight, token, up, gated, out_w, out, layer, all_grad, total
):
    grad_ref = grad_in.ready()
    heads = grad_ref.shape[0]
    head = grad_ref.shape[2] // 3
    width = heads * head
    all_grad[:, :width] = gate_grad.ready()[...]
    for index in range(heads):
        for part in range(3):
            start = (part + 1) * width + index * head
            all_grad[:, start : start + head] = grad_ref[index, :, part * head : (part + 1) * head]
    for step in range(width // TILE):
        part = slice(step * TILE, (step + 1) * TILE)
        weight.wait(step)
        total[:, part] = dot_nt(all_grad[...], weight.near[part, :])
    grad = total[...]
    normed, inverse = layer_norm(token.ready()[...].astype(F32))
    first = jnp.mean(grad, axis=-1, keepdims=True)
    second = jnp.mean(grad * normed, axis=-1, keepdims=True)
    back = (grad - first - normed * second) * inverse
    out.ref[...] = (up.ready()[...].astype(F32) + back).astype(BF16)
    out.send()
    result = dot_nn(gated.ready()[...], out_w.ready()[...])
    layer.ref[...] = (token.ready()[...].astype(F32) + result).astype(BF16)


def shift(values, by):
    return lax.ppermute(values, "seq", [(index, (index + by) % 8) for index in range(8)])


def swap(values, axis, bits, size):
    return lax.ppermute(values, axis, [(index, index ^ bits) for index in range(size)])


def gather_first(own):
    return swap(own, "seq", 1, 8), shift(own, -2), shift(own, 2)


def gather_rest(own, mate, after, before):
    half = own.shape[0] // 2
    across_low = shift(after[:half], -2)
    across_high = shift(before[half:], 2)
    mate_before = swap(before, "seq", 1, 8)
    mate_after = shift(mate, -2)
    mate_across_low = swap(across_low, "seq", 1, 8)
    mate_across_high = shift(mate_before[half:], 2)
    me = lax.axis_index("seq").astype(jnp.int32)
    other = me ^ 1
    pieces = [
        (own, me, 0),
        (mate, other, 0),
        (after, me + 2, 0),
        (before, me + 6, 0),
        (across_low, me + 4, 0),
        (across_high, me + 4, half),
        (mate_before, other + 6, 0),
        (mate_after, other + 2, 0),
        (mate_across_low, other + 4, 0),
        (mate_across_high, other + 4, half),
    ]
    starts = [(place % 8) * own.shape[0] + first for _, place, first in pieces]
    return [piece for piece, _, _ in pieces], starts


PIECES = 10
HALF = TILE // 2


CHIPS = [
    [place * 8 + part for place in range(core, 16, 2) for part in range(8)] for core in range(2)
]


def exchange_chips(values):
    return lax.all_to_all(values, ("dp", "seq"), 0, 0, axis_index_groups=CHIPS)


def exchange(values):
    return lax.all_to_all(values, "seq", 0, 0)


def per_device(tokens, proj_weight, out_weight, rel_bias, segment_ids, distance_bucket, out_grad):
    heads, buckets = rel_bias.shape
    rows, width = tokens.shape[1:]
    head = width // heads
    length = segment_ids.shape[1]
    scale = head ** (-0.5)
    reach = 1024 // TILE
    me = lax.axis_index("seq").astype(jnp.int32)
    core = (lax.axis_index("dp") % 2).astype(jnp.int32)
    token_row = tokens[0]
    upstream = out_grad[0]

    half = call(
        norm_kernel, [shape((rows, width), BF16)], "norm"
    )(token_row)[0]
    near = gather_first(half)

    gg, gate_proj, weight = call(
        prepare_kernel,
        [shape((rows, width), F32), shape((rows, width), F32), shape((width, 3 * head), BF16)],
        "prepare",
        smem=1,
        far=(4,),
        scratch=[pltpu.VMEM((width, width), BF16), pltpu.SemaphoreType.DMA((4,))],
        flops=4 * rows * width * width,
    )(me[None], upstream, half, out_weight, proj_weight)
    one_hot = (
        distance_bucket[None, : reach * TILE] == jnp.arange(buckets, dtype=jnp.int32)[:, None]
    ).astype(F32)
    table = jnp.dot(
        lax.dynamic_slice_in_dim(rel_bias, me, 1, 0),
        one_hot,
        precision=lax.Precision.HIGHEST,
        preferred_element_type=F32,
    )
    mask = (segment_ids[0][:, None] == jnp.arange(128, dtype=jnp.int32)[None, :]).astype(BF16)
    near, gg, gate_proj, weight, table, mask = lax.optimization_barrier(
        (near, gg, gate_proj, weight, table, mask)
    )
    pieces, starts = gather_rest(half, *near)
    info = lax.optimization_barrier(jnp.stack(starts + [core]))

    tiles = pltpu.VMEM((reach + 1, TILE, TILE), F32)
    features, slopes, attended = call(
        functools.partial(forward_kernel, scale),
        [
            shape((length, 3 * head), BF16),
            shape((length, 3 * head), BF16),
            shape((8, rows + 16, head), BF16),
        ],
        "forward",
        smem=1,
        out_parts={2: 8},
        scratch=[tiles, pltpu.VMEM((length, 2 * head), BF16)],
        flops=2 * length * width * 4 * head,
    )(info, weight, table, mask, *pieces)
    attended_own = exchange(attended)

    row_shape = shape((rows, width), BF16)
    send, gate_grad, gated = call(
        mix_kernel,
        [shape((heads, rows, 2 * head), BF16), row_shape, row_shape],
        "mix",
    )(attended_own, gate_proj, gg)
    mix_head = exchange(send)

    grads = call(
        functools.partial(backward_kernel, scale),
        [shape((8, rows, 3 * head), BF16)],
        "backward",
        parts={1: 4, 2: 4, 3: 4},
        out_parts={0: 2},
        scratch=[
            pltpu.VMEM((length, head), F32),
            pltpu.VMEM((length, head), F32),
            tiles,
            pltpu.VMEM((length, 2 * head), BF16),
        ],
        flops=10 * length * 4096 * head,
    )(table, mask, features, mix_head, slopes)[0]
    grads_own = exchange(grads)

    cells = shape((8, width // 16, 4 * head + width), BF16)
    third = shape((8, width // 16, 4 * head), BF16)
    mine, first, second, last = call(
        sums_kernel,
        [cells, third, third, third],
        "sums",
        smem=1,
        scratch=[pltpu.VMEM((length, 4 * head), BF16)],
        flops=2 * length * width * 4 * head + 2 * rows * width * width,
    )(info, mix_head, grads, *pieces, gated, upstream)
    others = [swap(part, "dp", 1, 16) for part in (first, second, last)]
    both = call(join_kernel, [cells], "join", light=True, limit=16)(mine, *others)[0]
    both, grads_own = lax.optimization_barrier((both, grads_own))
    few = width // 128
    parts = exchange_chips(both.reshape(64, few, 4 * head + width))
    final = jnp.sum(parts.reshape(8, 8, few, -1).astype(F32), axis=0)
    proj_out = final[:, :, : 4 * head].reshape(8, few, 4, head)
    proj_out = proj_out.transpose(1, 2, 0, 3).reshape(few, 4 * width)
    out_out = jnp.sum(final[:, :, 4 * head :], axis=0)

    grad_row, layer_row = call(
        input_kernel,
        [row_shape, row_shape],
        "input_grad",
        parts={2: width // TILE},
        scratch=[pltpu.VMEM((rows, 4 * width), BF16), pltpu.VMEM((rows, width), F32)],
        flops=8 * rows * width * width,
    )(gate_grad, grads_own, proj_weight, token_row, upstream, gated, out_weight)
    return layer_row[None], grad_row[None], proj_out, out_out


def solution(mesh):
    return jax.shard_map(
        per_device,
        mesh=mesh,
        in_specs=(P("dp", "seq", None), P(), P(), P(), P("dp", None), P(), P("dp", "seq", None)),
        out_specs=(
            P("dp", "seq", None),
            P("dp", "seq", None),
            P(("dp", "seq"), None),
            P(("dp", "seq"), None),
        ),
        check_vma=False,
    )
```

```python
import functools
import jax
import jax.numpy as jnp
from jax import lax
from jax.experimental import pallas as pl
from jax.experimental.pallas import tpu as pltpu
from jax.sharding import PartitionSpec as P

EPS = 1e-05
TILE = 256
DEAD = -1e30
F32 = jnp.float32
BF16 = jnp.bfloat16


def layer_norm(values):
    average = jnp.mean(values, axis=-1, keepdims=True)
    centered = values - average
    inverse = lax.rsqrt(jnp.mean(centered * centered, axis=-1, keepdims=True) + EPS)
    return centered * inverse, inverse


def dot_nn(left, right):
    return lax.dot_general(left, right, (((1,), (0,)), ((), ())), preferred_element_type=F32)


def dot_nt(left, right):
    return lax.dot_general(left, right, (((1,), (1,)), ((), ())), preferred_element_type=F32)


def dot_tn(left, right):
    return lax.dot_general(left, right, (((0,), (0,)), ((), ())), preferred_element_type=F32)


class Incoming:
    def __init__(self, far, near, sems, first, parts):
        self.near = near
        self.size = near.shape[0] // parts
        self.copies = []
        for part in range(parts):
            rows = pl.ds(part * self.size, self.size)
            self.copies.append(
                pltpu.make_async_copy(far.at[rows], near.at[rows], sems.at[first + part])
            )
        self.pending = [True] * parts

    def start(self, part):
        if part < len(self.copies):
            self.copies[part].start()

    def wait(self, part):
        if part < len(self.copies) and self.pending[part]:
            self.copies[part].wait()
            self.pending[part] = False

    def ready(self):
        for part in range(len(self.copies)):
            self.wait(part)
        return self.near


class Outgoing:
    def __init__(self, near, far, sems, first, parts):
        self.ref = near
        size = near.shape[0] // parts
        self.copies = []
        for part in range(parts):
            rows = pl.ds(part * size, size)
            self.copies.append(
                pltpu.make_async_copy(near.at[rows], far.at[rows], sems.at[first + part])
            )
        self.sent = [False] * parts

    def send(self, part=None):
        if part is not None and len(self.copies) == 1:
            return
        for index, copy in enumerate(self.copies):
            if part in (None, index) and not self.sent[index]:
                copy.start()
                self.sent[index] = True

    def finish(self):
        for copy in self.copies:
            copy.wait()


def call(body, outs, name, smem=0, scratch=(), flops=0, far=(), parts=None, out_parts=None, limit=58, light=False):
    parts = parts or {}
    out_parts = out_parts or {}

    def run(*args):
        size = sum(a.size * a.dtype.itemsize for a in args)
        size += sum(o.size * o.dtype.itemsize for o in outs)
        near_in = [i for i in range(smem, len(args)) if i not in far]
        counts = [parts.get(i, 1) for i in near_in]
        kept = [pltpu.VMEM(args[i].shape, args[i].dtype) for i in near_in]
        kept += [pltpu.VMEM(out.shape, out.dtype) for out in outs]
        out_counts = [out_parts.get(i, 1) for i in range(len(outs))]
        kept += [pltpu.SemaphoreType.DMA((sum(counts),)), pltpu.SemaphoreType.DMA((sum(out_counts),))]

        def kernel(*refs):
            ins, refs = refs[: len(args)], refs[len(args) :]
            far_outs, refs = refs[: len(outs)], refs[len(outs) :]
            near, refs = refs[: len(near_in)], refs[len(near_in) :]
            near_outs, refs = refs[: len(outs)], refs[len(outs) :]
            in_sems, out_sems, extra = refs[0], refs[1], refs[2:]
            values = list(ins)
            first = 0
            for place, ref, count in zip(near_in, near, counts):
                values[place] = Incoming(ins[place], ref, in_sems, first, count)
                first += count
            for part in range(max(counts)):
                for place in near_in:
                    values[place].start(part)
            results = []
            first = 0
            for ref, away, count in zip(near_outs, far_outs, out_counts):
                results.append(Outgoing(ref, away, out_sems, first, count))
                first += count
            body(*values, *results, *extra)
            for place in near_in:
                values[place].ready()
            for result in results:
                result.send()
            for result in results:
                result.finish()

        return pl.pallas_call(
            kernel,
            out_shape=outs,
            in_specs=[pl.BlockSpec(memory_space=pltpu.SMEM)] * smem
            + [pl.BlockSpec(memory_space=pltpu.HBM)] * (len(args) - smem),
            out_specs=[pl.BlockSpec(memory_space=pltpu.HBM)] * len(outs),
            scratch_shapes=kept + list(scratch),
            compiler_params=pltpu.CompilerParams(vmem_limit_bytes=limit * 1024 * 1024),
            cost_estimate=pl.CostEstimate(flops=flops, bytes_accessed=0 if light else size, transcendentals=0),
            name=name,
        )(*args)

    return run


def shape(dims, kind):
    return jax.ShapeDtypeStruct(dims, kind)


def norm_kernel(token, half):
    for part in range(len(token.copies)):
        token.wait(part)
        rows = slice(part * token.size, (part + 1) * token.size)
        normed, _ = layer_norm(token.near[rows, :].astype(F32))
        half.ref[rows, :] = normed.astype(BF16)
        half.send(part)


def prepare_kernel(me_smem, up, half, out_w, weight_far, gg, gate, weight, gate_w, sems):
    width = gate_w.shape[0]
    head = weight.ref.shape[1] // 3
    copies = [pltpu.make_async_copy(weight_far.at[:, :width], gate_w, sems.at[0])]
    for part in range(3):
        start = pl.multiple_of((part + 1) * width + me_smem[0] * head, head)
        source = weight_far.at[:, pl.ds(start, head)]
        target = weight.ref.at[:, part * head : (part + 1) * head]
        copies.append(pltpu.make_async_copy(source, target, sems.at[part + 1]))
    for copy in copies:
        copy.start()
    gg.ref[...] = dot_nt(up.ready()[...], out_w.ready()[...])
    gg.send()
    copies[0].wait()
    gate.ref[...] = dot_nn(half.ready()[...], gate_w[...])
    gate.send()
    for copy in copies[1:]:
        copy.wait()


def bias_tiles(table_ref, tile_ref, turned):
    count = tile_ref.shape[0]
    key_at = lax.broadcasted_iota(jnp.int32, (TILE, TILE), 0)
    query_at = lax.broadcasted_iota(jnp.int32, (TILE, TILE), 1)
    for step in range(count):
        if step < count - 1:
            later = table_ref[:, step * TILE : (step + 1) * TILE]
        else:
            later = jnp.zeros((1, TILE), F32)
        if step > 0:
            earlier = table_ref[:, (step - 1) * TILE : step * TILE]
        else:
            earlier = jnp.zeros((1, TILE), F32)
        window = jnp.broadcast_to(jnp.concatenate([later, earlier], axis=1), (TILE, 2 * TILE))
        rolled = 0.5 * pltpu.roll(window, 0, 1, stride=1, stride_axis=0)[:, :TILE]
        if step == 0:
            rolled = jnp.where(key_at <= query_at, rolled, DEAD)
        tile_ref[step] = rolled if turned else rolled.T


def key_mask(mask):
    return ((1.0 - mask.astype(F32)) * DEAD).astype(BF16)


def project(values, weight):
    half = 0.5 * dot_nn(values, weight)
    lean = jnp.tanh(half)
    rise = 1.0 + lean
    slope = 0.5 * rise * (1.0 + half * (1.0 - lean))
    return (half * rise).astype(BF16), slope.astype(BF16)


def early_kernel(weight, *refs):
    pieces, (feature, slope) = refs[:EARLY], refs[EARLY:]
    weight_ref = weight.ready()
    for index, piece in enumerate(pieces):
        rows = slice(index * TILE, (index + 1) * TILE)
        made, rate = project(piece.ready()[...], weight_ref[...])
        feature.ref[rows, :] = made
        slope.ref[rows, :] = rate


def forward_kernel(scale, start_smem, *refs):
    weight, table, mask, feature_early, slope_early = refs[:5]
    pieces = refs[5 : PIECES - EARLY + 5]
    feature, slope, attended, bias_ref, key_ref, sems = refs[PIECES - EARLY + 5 :]
    feature_ref, slope_ref = feature.ref, slope.ref
    count, _, head = attended.ref.shape
    reach = bias_ref.shape[0] - 1
    copies = []
    for index in range(EARLY):
        source = pl.ds(index * TILE, TILE)
        rows = pl.ds(pl.multiple_of(start_smem[index], HALF), TILE)
        for far, near in ((feature_early, feature_ref), (slope_early, slope_ref)):
            copies.append(
                pltpu.make_async_copy(far.at[source], near.at[rows], sems.at[len(copies)])
            )
    for copy in copies:
        copy.start()
    row_at = lax.broadcasted_iota(jnp.int32, (16, HALF), 0)
    bias_tiles(table.ready(), bias_ref, False)
    mask_ref = mask.ready()
    key_ref[:, head:] = key_mask(mask_ref[...])
    weight_ref = weight.ready()
    for index, piece in enumerate(pieces):
        ref = piece.ready()
        rows = pl.ds(pl.multiple_of(start_smem[index + EARLY], HALF), ref.shape[0])
        made, rate = project(ref[...], weight_ref[...])
        feature_ref[rows, :] = made
        slope_ref[rows, :] = rate
    for copy in copies:
        copy.wait()
    feature.send()
    slope.send()
    key_ref[:, :head] = feature_ref[:, 2 * head :]
    for q_block in range(count):
        rows = slice(q_block * TILE, (q_block + 1) * TILE)
        query = jnp.concatenate([feature_ref[rows, head : 2 * head], mask_ref[rows, :]], axis=1)
        total = jnp.zeros((TILE, head), F32)
        for k_block in range(max(0, q_block - reach), q_block + 1):
            k_rows = slice(k_block * TILE, (k_block + 1) * TILE)
            half = dot_nt(query, key_ref[k_rows, :]) * (0.5 * scale) + bias_ref[q_block - k_block]
            weights = half * (1.0 + jnp.tanh(half))
            total = total + dot_nn(weights.astype(BF16), feature_ref[k_rows, :head])
        average = jnp.mean(total, axis=1, keepdims=True)
        attended.ref[q_block, :TILE, :] = (total - average).astype(BF16)
        wide = jnp.broadcast_to(average, total.shape).T[:16, :]
        high = wide.astype(BF16).astype(F32)
        low = wide - high
        packed = jnp.where(row_at == 0, high[:, :HALF], high[:, HALF:])
        packed = jnp.where(row_at == 2, low[:, :HALF], packed)
        packed = jnp.where(row_at == 3, low[:, HALF:], packed)
        attended.ref[q_block, TILE:, :] = packed.astype(BF16)
        attended.send(q_block)


def split_cells(core, total, cell):
    low = [total[2 * k * cell : (2 * k + 1) * cell] for k in range(2)]
    high = [total[(2 * k + 1) * cell : (2 * k + 2) * cell] for k in range(2)]
    mine = [jnp.where(core == 0, x, y) for x, y in zip(low, high)]
    other = [jnp.where(core == 0, y, x) for x, y in zip(low, high)]
    return mine, other


def mix_kernel(
    attended_in, gate_in, gg_in, send_out, gate_grad_out, gated_out
):
    attended_ref = attended_in.ready()
    send_ref = send_out.ref
    heads, _, head = attended_ref.shape
    rows = []
    for index in range(heads):
        packed = attended_ref[index, TILE:, :].astype(F32)
        rows.append(
            jnp.concatenate([packed[0:1] + packed[2:3], packed[1:2] + packed[3:4]], axis=1)
        )
    averages = jnp.concatenate(rows, axis=0).T
    attended = jnp.concatenate(
        [
            attended_ref[index, :TILE, :].astype(F32) + averages[:, index : index + 1]
            for index in range(heads)
        ],
        axis=1,
    )
    mixed, inverse = layer_norm(attended)
    half = 0.5 * gate_in.ready()[...]
    lean = jnp.tanh(half)
    rise = 1.0 + lean
    gate = (half * rise).astype(BF16).astype(F32)
    gg = gg_in.ready()[...]
    gated_out.ref[...] = (mixed * gate).astype(BF16)
    gate_grad = (gg * mixed * (0.5 * rise * (1.0 + half * (1.0 - lean)))).astype(BF16)
    gate_grad_out.ref[...] = gate_grad
    gate_grad_out.send()
    grad = gg * gate
    first = jnp.mean(grad, axis=-1, keepdims=True)
    second = jnp.mean(grad * mixed, axis=-1, keepdims=True)
    grad = ((grad - first - mixed * second) * inverse).astype(BF16)
    for index in range(heads):
        columns = slice(index * head, (index + 1) * head)
        send_ref[index, :, :head] = grad[:, columns]
        send_ref[index, :, head:] = gate_grad[:, columns]


def backward_kernel(
    scale, table, mask, feature, grad_in, slope_in, out, key_sum, value_sum, bias_ref, key_ref
):
    head = key_sum.shape[1]
    out_ref = out.ref
    bias_tiles(table.ready(), bias_ref, True)
    mask_ref, feature_ref = mask.near, feature.near
    grad_ref, slope_ref = grad_in.near, slope_in.near
    count = grad_ref.shape[0]
    reach = bias_ref.shape[0] - 1
    for q_block in range(count):
        rows = slice(q_block * TILE, (q_block + 1) * TILE)
        if q_block % 2 == 0:
            for source in (mask, feature, grad_in):
                source.wait(q_block // 2)
        key_ref[rows, :head] = feature_ref[rows, 2 * head :]
        key_ref[rows, head:] = key_mask(mask_ref[rows, :])
        query_half = feature_ref[rows, head : 2 * head]
        query = jnp.concatenate([query_half, mask_ref[rows, :]], axis=1)
        upstream = grad_ref[q_block, :, :head]
        total = jnp.zeros((TILE, head), F32)
        for k_block in range(max(0, q_block - reach), q_block + 1):
            k_rows = slice(k_block * TILE, (k_block + 1) * TILE)
            key_half = feature_ref[k_rows, 2 * head :]
            half = dot_nt(key_ref[k_rows, :], query) * (0.5 * scale) + bias_ref[q_block - k_block]
            lean = jnp.tanh(half)
            rise = 1.0 + lean
            weight = (half * rise).astype(BF16)
            grad_weight = dot_nt(feature_ref[k_rows, :head], upstream)
            grad_score = (grad_weight * (rise * (1.0 + half * (1.0 - lean)))).astype(BF16)
            value_term = dot_nn(weight, upstream)
            key_term = dot_nn(grad_score, query_half)
            if q_block == k_block:
                value_sum[k_rows, :] = value_term
                key_sum[k_rows, :] = key_term
            else:
                value_sum[k_rows, :] += value_term
                key_sum[k_rows, :] += key_term
            total = total + dot_tn(grad_score, key_half)
        slope_in.wait(q_block)
        slope = slope_ref[rows, head : 2 * head].astype(F32)
        out_ref[q_block, :, head : 2 * head] = (total * (0.5 * scale) * slope).astype(BF16)
        done = [q_block - reach] if q_block < count - 1 else range(q_block - reach, count)
        for block in done:
            if block < 0:
                continue
            rows = slice(block * TILE, (block + 1) * TILE)
            value_slope = slope_ref[rows, :head].astype(F32)
            key_slope = slope_ref[rows, 2 * head :].astype(F32)
            out_ref[block, :, :head] = (value_sum[rows, :] * value_slope).astype(BF16)
            key_grad = key_sum[rows, :] * (0.5 * scale) * key_slope
            out_ref[block, :, 2 * head :] = key_grad.astype(BF16)
            if block == count // 2 - 1:
                out.send(0)


def sums_kernel(info_smem, *refs):
    mix, grad = refs[:2]
    pieces = refs[2 : PIECES + 2]
    gated, up, mine_out = refs[PIECES + 2 : PIECES + 5]
    others, right_ref = refs[PIECES + 5 : -1], refs[-1]
    core = info_smem[PIECES]
    cell = TILE // 4
    mix_ref, grad_ref = mix.ready(), grad.ready()
    head = grad_ref.shape[2] // 3
    for block in range(grad_ref.shape[0]):
        rows = slice(block * TILE, (block + 1) * TILE)
        right_ref[rows, :head] = mix_ref[block, :, head:]
        right_ref[rows, head:] = grad_ref[block]
    for chunk in range(pieces[0].near.shape[1] // TILE):
        columns = slice(chunk * TILE, (chunk + 1) * TILE)
        total = jnp.zeros((TILE, 4 * head), F32)
        for index, piece in enumerate(pieces):
            ref = piece.ready()
            rows = pl.ds(pl.multiple_of(info_smem[index], HALF), ref.shape[0])
            total = total + dot_tn(ref[:, columns], right_ref[rows, :])
        mine, other = split_cells(core, total, cell)
        for index in range(2):
            mine_out.ref[2 * chunk + index, :, : 4 * head] = mine[index].astype(BF16)
            others[0].ref[2 * chunk + index] = other[index].astype(BF16)
    others[0].send()
    gated_ref = gated.ready()
    up_rows = up.ready()[...]
    for chunk in range(gated_ref.shape[1] // TILE):
        total = dot_tn(gated_ref[:, chunk * TILE : (chunk + 1) * TILE], up_rows)
        mine, other = split_cells(core, total, cell)
        for index in range(2):
            mine_out.ref[2 * chunk + index, :, 4 * head :] = mine[index].astype(BF16)
            for out, first in zip(others[1:], (0, 4 * head)):
                columns = slice(first, first + 4 * head)
                out.ref[2 * chunk + index] = other[index][:, columns].astype(BF16)
    mine_out.send()
    for out in others[1:]:
        out.send()


def join_kernel(mine, *refs):
    others, out = refs[:-1], refs[-1]
    mine_ref = mine.ready()
    first = 0
    for other in others:
        ref = other.ready()
        columns = slice(first, first + ref.shape[2])
        total = mine_ref[:, :, columns].astype(F32) + ref[...].astype(F32)
        out.ref[:, :, columns] = total.astype(BF16)
        first += ref.shape[2]


def input_kernel(
    gate_grad, grad_in, weight, token, up, gated, out_w, out, layer, all_grad, total
):
    grad_ref = grad_in.ready()
    heads = grad_ref.shape[0]
    head = grad_ref.shape[2] // 3
    width = heads * head
    all_grad[:, :width] = gate_grad.ready()[...]
    for index in range(heads):
        for part in range(3):
            start = (part + 1) * width + index * head
            all_grad[:, start : start + head] = grad_ref[index, :, part * head : (part + 1) * head]
    for step in range(width // TILE):
        part = slice(step * TILE, (step + 1) * TILE)
        weight.wait(step)
        total[:, part] = dot_nt(all_grad[...], weight.near[part, :])
    grad = total[...]
    normed, inverse = layer_norm(token.ready()[...].astype(F32))
    first = jnp.mean(grad, axis=-1, keepdims=True)
    second = jnp.mean(grad * normed, axis=-1, keepdims=True)
    back = (grad - first - normed * second) * inverse
    out.ref[...] = (up.ready()[...].astype(F32) + back).astype(BF16)
    out.send()
    result = dot_nn(gated.ready()[...], out_w.ready()[...])
    layer.ref[...] = (token.ready()[...].astype(F32) + result).astype(BF16)


def shift(values, by):
    return lax.ppermute(values, "seq", [(index, (index + by) % 8) for index in range(8)])


def swap(values, axis, bits, size):
    return lax.ppermute(values, axis, [(index, index ^ bits) for index in range(size)])


def gather_first(own):
    return swap(own, "seq", 1, 8), shift(own, -2), shift(own, 2)


def gather_rest(own, mate, after, before, early):
    half = own.shape[0] // 2
    across_low = shift(after[:half], -2)
    across_high = shift(before[half:], 2)
    mate_before = swap(before, "seq", 1, 8)
    mate_before, early = lax.optimization_barrier((mate_before, early))
    mate_after = shift(mate, -2)
    mate_across_low = swap(across_low, "seq", 1, 8)
    mate_across_high = shift(mate_before[half:], 2)
    me = lax.axis_index("seq").astype(jnp.int32)
    other = me ^ 1
    pieces = [
        (own, me, 0),
        (mate, other, 0),
        (after, me + 2, 0),
        (before, me + 6, 0),
        (across_low, me + 4, 0),
        (across_high, me + 4, half),
        (mate_before, other + 6, 0),
        (mate_after, other + 2, 0),
        (mate_across_low, other + 4, 0),
        (mate_across_high, other + 4, half),
    ]
    starts = [(place % 8) * own.shape[0] + first for _, place, first in pieces]
    return [piece for piece, _, _ in pieces], starts, early


PIECES = 10
EARLY = 4
HALF = TILE // 2


CHIPS = [
    [place * 8 + part for place in range(core, 16, 2) for part in range(8)] for core in range(2)
]


def exchange_chips(values):
    return lax.all_to_all(values, ("dp", "seq"), 0, 0, axis_index_groups=CHIPS)


def exchange(values):
    return lax.all_to_all(values, "seq", 0, 0)


def per_device(tokens, proj_weight, out_weight, rel_bias, segment_ids, distance_bucket, out_grad):
    heads, buckets = rel_bias.shape
    rows, width = tokens.shape[1:]
    head = width // heads
    length = segment_ids.shape[1]
    scale = head ** (-0.5)
    reach = 1024 // TILE
    me = lax.axis_index("seq").astype(jnp.int32)
    core = (lax.axis_index("dp") % 2).astype(jnp.int32)
    token_row = tokens[0]
    upstream = out_grad[0]

    half = call(
        norm_kernel, [shape((rows, width), BF16)], "norm"
    )(token_row)[0]
    near = gather_first(half)

    gg, gate_proj, weight = call(
        prepare_kernel,
        [shape((rows, width), F32), shape((rows, width), F32), shape((width, 3 * head), BF16)],
        "prepare",
        smem=1,
        far=(4,),
        scratch=[pltpu.VMEM((width, width), BF16), pltpu.SemaphoreType.DMA((4,))],
        flops=4 * rows * width * width,
    )(me[None], upstream, half, out_weight, proj_weight)
    one_hot = (
        distance_bucket[None, : reach * TILE] == jnp.arange(buckets, dtype=jnp.int32)[:, None]
    ).astype(F32)
    table = jnp.dot(
        lax.dynamic_slice_in_dim(rel_bias, me, 1, 0),
        one_hot,
        precision=lax.Precision.HIGHEST,
        preferred_element_type=F32,
    )
    mask = (segment_ids[0][:, None] == jnp.arange(128, dtype=jnp.int32)[None, :]).astype(BF16)
    near, gg, gate_proj, weight, table, mask = lax.optimization_barrier(
        (near, gg, gate_proj, weight, table, mask)
    )
    kept = shape((EARLY * rows, 3 * head), BF16)
    early = call(early_kernel, [kept, kept], "early", light=True)(weight, half, *near)
    pieces, starts, early = gather_rest(half, *near, early)
    info = lax.optimization_barrier(jnp.stack(starts + [core]))

    tiles = pltpu.VMEM((reach + 1, TILE, TILE), F32)
    features, slopes, attended = call(
        functools.partial(forward_kernel, scale),
        [
            shape((length, 3 * head), BF16),
            shape((length, 3 * head), BF16),
            shape((8, rows + 16, head), BF16),
        ],
        "forward",
        smem=1,
        out_parts={2: 8},
        far=(4, 5),
        scratch=[
            tiles, pltpu.VMEM((length, 2 * head), BF16), pltpu.SemaphoreType.DMA((2 * EARLY,))
        ],
        flops=2 * length * width * 4 * head,
    )(info, weight, table, mask, *early, *pieces[EARLY:])
    attended_own = exchange(attended)

    row_shape = shape((rows, width), BF16)
    send, gate_grad, gated = call(
        mix_kernel,
        [shape((heads, rows, 2 * head), BF16), row_shape, row_shape],
        "mix",
    )(attended_own, gate_proj, gg)
    mix_head = exchange(send)

    grads = call(
        functools.partial(backward_kernel, scale),
        [shape((8, rows, 3 * head), BF16)],
        "backward",
        parts={1: 4, 2: 4, 3: 4},
        out_parts={0: 2},
        scratch=[
            pltpu.VMEM((length, head), F32),
            pltpu.VMEM((length, head), F32),
            tiles,
            pltpu.VMEM((length, 2 * head), BF16),
        ],
        flops=10 * length * 4096 * head,
    )(table, mask, features, mix_head, slopes)[0]
    grads_own = exchange(grads)

    cells = shape((8, width // 16, 4 * head + width), BF16)
    third = shape((8, width // 16, 4 * head), BF16)
    mine, first, second, last = call(
        sums_kernel,
        [cells, third, third, third],
        "sums",
        smem=1,
        scratch=[pltpu.VMEM((length, 4 * head), BF16)],
        flops=2 * length * width * 4 * head + 2 * rows * width * width,
    )(info, mix_head, grads, *pieces, gated, upstream)
    others = [swap(part, "dp", 1, 16) for part in (first, second, last)]
    both = call(join_kernel, [cells], "join", light=True, limit=16)(mine, *others)[0]
    both, grads_own = lax.optimization_barrier((both, grads_own))
    few = width // 128
    parts = exchange_chips(both.reshape(64, few, 4 * head + width))
    final = jnp.sum(parts.reshape(8, 8, few, -1).astype(F32), axis=0)
    proj_out = final[:, :, : 4 * head].reshape(8, few, 4, head)
    proj_out = proj_out.transpose(1, 2, 0, 3).reshape(few, 4 * width)
    out_out = jnp.sum(final[:, :, 4 * head :], axis=0)

    grad_row, layer_row = call(
        input_kernel,
        [row_shape, row_shape],
        "input_grad",
        parts={2: width // TILE},
        scratch=[pltpu.VMEM((rows, 4 * width), BF16), pltpu.VMEM((rows, width), F32)],
        flops=8 * rows * width * width,
    )(gate_grad, grads_own, proj_weight, token_row, upstream, gated, out_weight)
    return layer_row[None], grad_row[None], proj_out, out_out


def solution(mesh):
    return jax.shard_map(
        per_device,
        mesh=mesh,
        in_specs=(P("dp", "seq", None), P(), P(), P(), P("dp", None), P(), P("dp", "seq", None)),
        out_specs=(
            P("dp", "seq", None),
            P("dp", "seq", None),
            P(("dp", "seq"), None),
            P(("dp", "seq"), None),
        ),
        check_vma=False,
    )
```

```python
import functools
import jax
import jax.numpy as jnp
from jax import lax
from jax.experimental import pallas as pl
from jax.experimental.pallas import tpu as pltpu
from jax.sharding import PartitionSpec as P

EPS = 1e-05
TILE = 256
DEAD = -1e30
F32 = jnp.float32
BF16 = jnp.bfloat16


def layer_norm(values):
    average = jnp.mean(values, axis=-1, keepdims=True)
    centered = values - average
    inverse = lax.rsqrt(jnp.mean(centered * centered, axis=-1, keepdims=True) + EPS)
    return centered * inverse, inverse


def dot_nn(left, right):
    return lax.dot_general(left, right, (((1,), (0,)), ((), ())), preferred_element_type=F32)


def dot_nt(left, right):
    return lax.dot_general(left, right, (((1,), (1,)), ((), ())), preferred_element_type=F32)


def dot_tn(left, right):
    return lax.dot_general(left, right, (((0,), (0,)), ((), ())), preferred_element_type=F32)


class Incoming:
    def __init__(self, far, near, sems, first, parts):
        self.near = near
        self.size = near.shape[0] // parts
        self.copies = []
        for part in range(parts):
            rows = pl.ds(part * self.size, self.size)
            self.copies.append(
                pltpu.make_async_copy(far.at[rows], near.at[rows], sems.at[first + part])
            )
        self.pending = [True] * parts

    def start(self, part):
        if part < len(self.copies):
            self.copies[part].start()

    def wait(self, part):
        if part < len(self.copies) and self.pending[part]:
            self.copies[part].wait()
            self.pending[part] = False

    def ready(self):
        for part in range(len(self.copies)):
            self.wait(part)
        return self.near


class Outgoing:
    def __init__(self, near, far, sems, first, parts):
        self.ref = near
        size = near.shape[0] // parts
        self.copies = []
        for part in range(parts):
            rows = pl.ds(part * size, size)
            self.copies.append(
                pltpu.make_async_copy(near.at[rows], far.at[rows], sems.at[first + part])
            )
        self.sent = [False] * parts

    def send(self, part=None):
        if part is not None and len(self.copies) == 1:
            return
        for index, copy in enumerate(self.copies):
            if part in (None, index) and not self.sent[index]:
                copy.start()
                self.sent[index] = True

    def finish(self):
        for copy in self.copies:
            copy.wait()


def call(body, outs, name, smem=0, scratch=(), flops=0, far=(), parts=None, out_parts=None, limit=58, light=False):
    parts = parts or {}
    out_parts = out_parts or {}

    def run(*args):
        size = sum(a.size * a.dtype.itemsize for a in args)
        size += sum(o.size * o.dtype.itemsize for o in outs)
        near_in = [i for i in range(smem, len(args)) if i not in far]
        counts = [parts.get(i, 1) for i in near_in]
        kept = [pltpu.VMEM(args[i].shape, args[i].dtype) for i in near_in]
        kept += [pltpu.VMEM(out.shape, out.dtype) for out in outs]
        out_counts = [out_parts.get(i, 1) for i in range(len(outs))]
        kept += [pltpu.SemaphoreType.DMA((sum(counts),)), pltpu.SemaphoreType.DMA((sum(out_counts),))]

        def kernel(*refs):
            ins, refs = refs[: len(args)], refs[len(args) :]
            far_outs, refs = refs[: len(outs)], refs[len(outs) :]
            near, refs = refs[: len(near_in)], refs[len(near_in) :]
            near_outs, refs = refs[: len(outs)], refs[len(outs) :]
            in_sems, out_sems, extra = refs[0], refs[1], refs[2:]
            values = list(ins)
            first = 0
            for place, ref, count in zip(near_in, near, counts):
                values[place] = Incoming(ins[place], ref, in_sems, first, count)
                first += count
            for part in range(max(counts)):
                for place in near_in:
                    values[place].start(part)
            results = []
            first = 0
            for ref, away, count in zip(near_outs, far_outs, out_counts):
                results.append(Outgoing(ref, away, out_sems, first, count))
                first += count
            body(*values, *results, *extra)
            for place in near_in:
                values[place].ready()
            for result in results:
                result.send()
            for result in results:
                result.finish()

        return pl.pallas_call(
            kernel,
            out_shape=outs,
            in_specs=[pl.BlockSpec(memory_space=pltpu.SMEM)] * smem
            + [pl.BlockSpec(memory_space=pltpu.HBM)] * (len(args) - smem),
            out_specs=[pl.BlockSpec(memory_space=pltpu.HBM)] * len(outs),
            scratch_shapes=kept + list(scratch),
            compiler_params=pltpu.CompilerParams(vmem_limit_bytes=limit * 1024 * 1024),
            cost_estimate=pl.CostEstimate(flops=flops, bytes_accessed=0 if light else size, transcendentals=0),
            name=name,
        )(*args)

    return run


def shape(dims, kind):
    return jax.ShapeDtypeStruct(dims, kind)


def norm_kernel(token, half):
    for part in range(len(token.copies)):
        token.wait(part)
        rows = slice(part * token.size, (part + 1) * token.size)
        normed, _ = layer_norm(token.near[rows, :].astype(F32))
        half.ref[rows, :] = normed.astype(BF16)
        half.send(part)


def prepare_kernel(me_smem, up, half, out_w, weight_far, gg, gate, weight, gate_w, sems):
    width = gate_w.shape[0]
    head = weight.ref.shape[1] // 3
    copies = [pltpu.make_async_copy(weight_far.at[:, :width], gate_w, sems.at[0])]
    for part in range(3):
        start = pl.multiple_of((part + 1) * width + me_smem[0] * head, head)
        source = weight_far.at[:, pl.ds(start, head)]
        target = weight.ref.at[:, part * head : (part + 1) * head]
        copies.append(pltpu.make_async_copy(source, target, sems.at[part + 1]))
    for copy in copies:
        copy.start()
    gg.ref[...] = dot_nt(up.ready()[...], out_w.ready()[...])
    gg.send()
    copies[0].wait()
    gate.ref[...] = dot_nn(half.ready()[...], gate_w[...])
    gate.send()
    for copy in copies[1:]:
        copy.wait()


def bias_tiles(table_ref, tile_ref, turned):
    count = tile_ref.shape[0]
    key_at = lax.broadcasted_iota(jnp.int32, (TILE, TILE), 0)
    query_at = lax.broadcasted_iota(jnp.int32, (TILE, TILE), 1)
    for step in range(count):
        if step < count - 1:
            later = table_ref[:, step * TILE : (step + 1) * TILE]
        else:
            later = jnp.zeros((1, TILE), F32)
        if step > 0:
            earlier = table_ref[:, (step - 1) * TILE : step * TILE]
        else:
            earlier = jnp.zeros((1, TILE), F32)
        window = jnp.broadcast_to(jnp.concatenate([later, earlier], axis=1), (TILE, 2 * TILE))
        rolled = 0.5 * pltpu.roll(window, 0, 1, stride=1, stride_axis=0)[:, :TILE]
        if step == 0:
            rolled = jnp.where(key_at <= query_at, rolled, DEAD)
        tile_ref[step] = rolled if turned else rolled.T


def key_mask(mask):
    return ((1.0 - mask.astype(F32)) * DEAD).astype(BF16)


def project(values, weight):
    half = 0.5 * dot_nn(values, weight)
    lean = jnp.tanh(half)
    rise = 1.0 + lean
    slope = 0.5 * rise * (1.0 + half * (1.0 - lean))
    return (half * rise).astype(BF16), slope.astype(BF16)


def early_kernel(weight, *refs):
    pieces, (feature, slope) = refs[:-2], refs[-2:]
    weight_ref = weight.ready()
    first = 0
    for piece in pieces:
        values = piece.ready()[...]
        rows = slice(first, first + values.shape[0])
        made, rate = project(values, weight_ref[...])
        feature.ref[rows, :] = made
        slope.ref[rows, :] = rate
        first += values.shape[0]


def forward_kernel(scale, start_smem, *refs):
    weight, table, mask = refs[:3]
    groups = ((refs[3], refs[4], SIZES[:EARLY]), (refs[5], refs[6], SIZES[EARLY:]))
    done = len(SIZES)
    pieces = refs[7 : PIECES - done + 7]
    feature, slope, attended, bias_ref, key_ref, sems = refs[PIECES - done + 7 :]
    feature_ref, slope_ref = feature.ref, slope.ref
    count, _, head = attended.ref.shape
    reach = bias_ref.shape[0] - 1
    copies = []
    index = 0
    for feature_far, slope_far, sizes in groups:
        first = 0
        for size in sizes:
            source = pl.ds(first, size)
            rows = pl.ds(pl.multiple_of(start_smem[index], HALF), size)
            for far, near in ((feature_far, feature_ref), (slope_far, slope_ref)):
                copies.append(
                    pltpu.make_async_copy(far.at[source], near.at[rows], sems.at[len(copies)])
                )
            first += size
            index += 1
    for copy in copies:
        copy.start()
    row_at = lax.broadcasted_iota(jnp.int32, (16, HALF), 0)
    bias_tiles(table.ready(), bias_ref, False)
    mask_ref = mask.ready()
    key_ref[:, head:] = key_mask(mask_ref[...])
    weight_ref = weight.ready()
    for index, piece in enumerate(pieces):
        ref = piece.ready()
        rows = pl.ds(pl.multiple_of(start_smem[index + done], HALF), ref.shape[0])
        made, rate = project(ref[...], weight_ref[...])
        feature_ref[rows, :] = made
        slope_ref[rows, :] = rate
    for copy in copies:
        copy.wait()
    feature.send()
    slope.send()
    key_ref[:, :head] = feature_ref[:, 2 * head :]
    for q_block in range(count):
        rows = slice(q_block * TILE, (q_block + 1) * TILE)
        query = jnp.concatenate([feature_ref[rows, head : 2 * head], mask_ref[rows, :]], axis=1)
        total = jnp.zeros((TILE, head), F32)
        for k_block in range(max(0, q_block - reach), q_block + 1):
            k_rows = slice(k_block * TILE, (k_block + 1) * TILE)
            half = dot_nt(query, key_ref[k_rows, :]) * (0.5 * scale) + bias_ref[q_block - k_block]
            weights = half * (1.0 + jnp.tanh(half))
            total = total + dot_nn(weights.astype(BF16), feature_ref[k_rows, :head])
        average = jnp.mean(total, axis=1, keepdims=True)
        attended.ref[q_block, :TILE, :] = (total - average).astype(BF16)
        wide = jnp.broadcast_to(average, total.shape).T[:16, :]
        high = wide.astype(BF16).astype(F32)
        low = wide - high
        packed = jnp.where(row_at == 0, high[:, :HALF], high[:, HALF:])
        packed = jnp.where(row_at == 2, low[:, :HALF], packed)
        packed = jnp.where(row_at == 3, low[:, HALF:], packed)
        attended.ref[q_block, TILE:, :] = packed.astype(BF16)
        attended.send(q_block)


def split_cells(core, total, cell):
    low = [total[2 * k * cell : (2 * k + 1) * cell] for k in range(2)]
    high = [total[(2 * k + 1) * cell : (2 * k + 2) * cell] for k in range(2)]
    mine = [jnp.where(core == 0, x, y) for x, y in zip(low, high)]
    other = [jnp.where(core == 0, y, x) for x, y in zip(low, high)]
    return mine, other


def mix_kernel(
    attended_in, gate_in, gg_in, send_out, gate_grad_out, gated_out
):
    attended_ref = attended_in.ready()
    send_ref = send_out.ref
    heads, _, head = attended_ref.shape
    rows = []
    for index in range(heads):
        packed = attended_ref[index, TILE:, :].astype(F32)
        rows.append(
            jnp.concatenate([packed[0:1] + packed[2:3], packed[1:2] + packed[3:4]], axis=1)
        )
    averages = jnp.concatenate(rows, axis=0).T
    attended = jnp.concatenate(
        [
            attended_ref[index, :TILE, :].astype(F32) + averages[:, index : index + 1]
            for index in range(heads)
        ],
        axis=1,
    )
    mixed, inverse = layer_norm(attended)
    half = 0.5 * gate_in.ready()[...]
    lean = jnp.tanh(half)
    rise = 1.0 + lean
    gate = (half * rise).astype(BF16).astype(F32)
    gg = gg_in.ready()[...]
    gated_out.ref[...] = (mixed * gate).astype(BF16)
    gate_grad = (gg * mixed * (0.5 * rise * (1.0 + half * (1.0 - lean)))).astype(BF16)
    gate_grad_out.ref[...] = gate_grad
    gate_grad_out.send()
    grad = gg * gate
    first = jnp.mean(grad, axis=-1, keepdims=True)
    second = jnp.mean(grad * mixed, axis=-1, keepdims=True)
    grad = ((grad - first - mixed * second) * inverse).astype(BF16)
    for index in range(heads):
        columns = slice(index * head, (index + 1) * head)
        send_ref[index, :, :head] = grad[:, columns]
        send_ref[index, :, head:] = gate_grad[:, columns]


def backward_kernel(
    scale, table, mask, feature, grad_in, slope_in, out, key_sum, value_sum, bias_ref, key_ref
):
    head = key_sum.shape[1]
    out_ref = out.ref
    bias_tiles(table.ready(), bias_ref, True)
    mask_ref, feature_ref = mask.near, feature.near
    grad_ref, slope_ref = grad_in.near, slope_in.near
    count = grad_ref.shape[0]
    reach = bias_ref.shape[0] - 1
    for q_block in range(count):
        rows = slice(q_block * TILE, (q_block + 1) * TILE)
        if q_block % 2 == 0:
            for source in (mask, feature, grad_in):
                source.wait(q_block // 2)
        key_ref[rows, :head] = feature_ref[rows, 2 * head :]
        key_ref[rows, head:] = key_mask(mask_ref[rows, :])
        query_half = feature_ref[rows, head : 2 * head]
        query = jnp.concatenate([query_half, mask_ref[rows, :]], axis=1)
        upstream = grad_ref[q_block, :, :head]
        total = jnp.zeros((TILE, head), F32)
        for k_block in range(max(0, q_block - reach), q_block + 1):
            k_rows = slice(k_block * TILE, (k_block + 1) * TILE)
            key_half = feature_ref[k_rows, 2 * head :]
            half = dot_nt(key_ref[k_rows, :], query) * (0.5 * scale) + bias_ref[q_block - k_block]
            lean = jnp.tanh(half)
            rise = 1.0 + lean
            weight = (half * rise).astype(BF16)
            grad_weight = dot_nt(feature_ref[k_rows, :head], upstream)
            grad_score = (grad_weight * (rise * (1.0 + half * (1.0 - lean)))).astype(BF16)
            value_term = dot_nn(weight, upstream)
            key_term = dot_nn(grad_score, query_half)
            if q_block == k_block:
                value_sum[k_rows, :] = value_term
                key_sum[k_rows, :] = key_term
            else:
                value_sum[k_rows, :] += value_term
                key_sum[k_rows, :] += key_term
            total = total + dot_tn(grad_score, key_half)
        slope_in.wait(q_block)
        slope = slope_ref[rows, head : 2 * head].astype(F32)
        out_ref[q_block, :, head : 2 * head] = (total * (0.5 * scale) * slope).astype(BF16)
        done = [q_block - reach] if q_block < count - 1 else range(q_block - reach, count)
        for block in done:
            if block < 0:
                continue
            rows = slice(block * TILE, (block + 1) * TILE)
            value_slope = slope_ref[rows, :head].astype(F32)
            key_slope = slope_ref[rows, 2 * head :].astype(F32)
            out_ref[block, :, :head] = (value_sum[rows, :] * value_slope).astype(BF16)
            key_grad = key_sum[rows, :] * (0.5 * scale) * key_slope
            out_ref[block, :, 2 * head :] = key_grad.astype(BF16)
            if block == count // 2 - 1:
                out.send(0)


def sums_kernel(info_smem, *refs):
    mix, grad = refs[:2]
    pieces = refs[2 : PIECES + 2]
    gated, up, mine_out = refs[PIECES + 2 : PIECES + 5]
    others, right_ref = refs[PIECES + 5 : -1], refs[-1]
    core = info_smem[PIECES]
    cell = TILE // 4
    mix_ref, grad_ref = mix.ready(), grad.ready()
    head = grad_ref.shape[2] // 3
    for block in range(grad_ref.shape[0]):
        rows = slice(block * TILE, (block + 1) * TILE)
        right_ref[rows, :head] = mix_ref[block, :, head:]
        right_ref[rows, head:] = grad_ref[block]
    for chunk in range(pieces[0].near.shape[1] // TILE):
        columns = slice(chunk * TILE, (chunk + 1) * TILE)
        total = jnp.zeros((TILE, 4 * head), F32)
        for index, piece in enumerate(pieces):
            ref = piece.ready()
            rows = pl.ds(pl.multiple_of(info_smem[index], HALF), ref.shape[0])
            total = total + dot_tn(ref[:, columns], right_ref[rows, :])
        mine, other = split_cells(core, total, cell)
        for index in range(2):
            mine_out.ref[2 * chunk + index, :, : 4 * head] = mine[index].astype(BF16)
            others[0].ref[2 * chunk + index] = other[index].astype(BF16)
    others[0].send()
    gated_ref = gated.ready()
    up_rows = up.ready()[...]
    for chunk in range(gated_ref.shape[1] // TILE):
        total = dot_tn(gated_ref[:, chunk * TILE : (chunk + 1) * TILE], up_rows)
        mine, other = split_cells(core, total, cell)
        for index in range(2):
            mine_out.ref[2 * chunk + index, :, 4 * head :] = mine[index].astype(BF16)
            for out, first in zip(others[1:], (0, 4 * head)):
                columns = slice(first, first + 4 * head)
                out.ref[2 * chunk + index] = other[index][:, columns].astype(BF16)
    mine_out.send()
    for out in others[1:]:
        out.send()


def join_kernel(mine, *refs):
    others, out = refs[:-1], refs[-1]
    mine_ref = mine.ready()
    first = 0
    for other in others:
        ref = other.ready()
        columns = slice(first, first + ref.shape[2])
        total = mine_ref[:, :, columns].astype(F32) + ref[...].astype(F32)
        out.ref[:, :, columns] = total.astype(BF16)
        first += ref.shape[2]


def input_kernel(
    gate_grad, grad_in, weight, token, up, gated, out_w, out, layer, all_grad, total
):
    grad_ref = grad_in.ready()
    heads = grad_ref.shape[0]
    head = grad_ref.shape[2] // 3
    width = heads * head
    all_grad[:, :width] = gate_grad.ready()[...]
    for index in range(heads):
        for part in range(3):
            start = (part + 1) * width + index * head
            all_grad[:, start : start + head] = grad_ref[index, :, part * head : (part + 1) * head]
    for step in range(width // TILE):
        part = slice(step * TILE, (step + 1) * TILE)
        weight.wait(step)
        total[:, part] = dot_nt(all_grad[...], weight.near[part, :])
    grad = total[...]
    normed, inverse = layer_norm(token.ready()[...].astype(F32))
    first = jnp.mean(grad, axis=-1, keepdims=True)
    second = jnp.mean(grad * normed, axis=-1, keepdims=True)
    back = (grad - first - normed * second) * inverse
    out.ref[...] = (up.ready()[...].astype(F32) + back).astype(BF16)
    out.send()
    result = dot_nn(gated.ready()[...], out_w.ready()[...])
    layer.ref[...] = (token.ready()[...].astype(F32) + result).astype(BF16)


def shift(values, by):
    return lax.ppermute(values, "seq", [(index, (index + by) % 8) for index in range(8)])


def swap(values, axis, bits, size):
    return lax.ppermute(values, axis, [(index, index ^ bits) for index in range(size)])


def gather_first(own):
    return swap(own, "seq", 1, 8), shift(own, -2), shift(own, 2)


def gather_rest(own, mate, after, before, early):
    half = own.shape[0] // 2
    across_low = shift(after[:half], -2)
    across_high = shift(before[half:], 2)
    mate_before = swap(before, "seq", 1, 8)
    mate_before, early = lax.optimization_barrier((mate_before, early))
    mate_after = shift(mate, -2)
    mate_across_low = swap(across_low, "seq", 1, 8)
    mate_across_high = shift(mate_before[half:], 2)
    me = lax.axis_index("seq").astype(jnp.int32)
    other = me ^ 1
    pieces = [
        (own, me, 0),
        (mate, other, 0),
        (after, me + 2, 0),
        (before, me + 6, 0),
        (across_low, me + 4, 0),
        (across_high, me + 4, half),
        (mate_before, other + 6, 0),
        (mate_after, other + 2, 0),
        (mate_across_low, other + 4, 0),
        (mate_across_high, other + 4, half),
    ]
    starts = [(place % 8) * own.shape[0] + first for _, place, first in pieces]
    return [piece for piece, _, _ in pieces], starts, early


PIECES = 10
EARLY = 4
SIZES = [256, 256, 256, 256, 128, 128, 256]
HALF = TILE // 2


CHIPS = [
    [place * 8 + part for place in range(core, 16, 2) for part in range(8)] for core in range(2)
]


def exchange_chips(values):
    return lax.all_to_all(values, ("dp", "seq"), 0, 0, axis_index_groups=CHIPS)


def exchange(values):
    return lax.all_to_all(values, "seq", 0, 0)


def per_device(tokens, proj_weight, out_weight, rel_bias, segment_ids, distance_bucket, out_grad):
    heads, buckets = rel_bias.shape
    rows, width = tokens.shape[1:]
    head = width // heads
    length = segment_ids.shape[1]
    scale = head ** (-0.5)
    reach = 1024 // TILE
    me = lax.axis_index("seq").astype(jnp.int32)
    core = (lax.axis_index("dp") % 2).astype(jnp.int32)
    token_row = tokens[0]
    upstream = out_grad[0]

    half = call(
        norm_kernel, [shape((rows, width), BF16)], "norm"
    )(token_row)[0]
    near = gather_first(half)

    gg, gate_proj, weight = call(
        prepare_kernel,
        [shape((rows, width), F32), shape((rows, width), F32), shape((width, 3 * head), BF16)],
        "prepare",
        smem=1,
        far=(4,),
        scratch=[pltpu.VMEM((width, width), BF16), pltpu.SemaphoreType.DMA((4,))],
        flops=4 * rows * width * width,
    )(me[None], upstream, half, out_weight, proj_weight)
    one_hot = (
        distance_bucket[None, : reach * TILE] == jnp.arange(buckets, dtype=jnp.int32)[:, None]
    ).astype(F32)
    table = jnp.dot(
        lax.dynamic_slice_in_dim(rel_bias, me, 1, 0),
        one_hot,
        precision=lax.Precision.HIGHEST,
        preferred_element_type=F32,
    )
    mask = (segment_ids[0][:, None] == jnp.arange(128, dtype=jnp.int32)[None, :]).astype(BF16)
    near, gg, gate_proj, weight, table, mask = lax.optimization_barrier(
        (near, gg, gate_proj, weight, table, mask)
    )
    kept = shape((EARLY * rows, 3 * head), BF16)
    kept_next = shape((2 * rows, 3 * head), BF16)
    early = call(early_kernel, [kept, kept], "early", light=True)(weight, half, *near)
    pieces, starts, early = gather_rest(half, *near, early)
    info = lax.optimization_barrier(jnp.stack(starts + [core]))
    later = call(early_kernel, [kept_next, kept_next], "later", light=True)(
        weight, *pieces[EARLY : len(SIZES)]
    )

    tiles = pltpu.VMEM((reach + 1, TILE, TILE), F32)
    features, slopes, attended = call(
        functools.partial(forward_kernel, scale),
        [
            shape((length, 3 * head), BF16),
            shape((length, 3 * head), BF16),
            shape((8, rows + 16, head), BF16),
        ],
        "forward",
        smem=1,
        out_parts={2: 8},
        far=(4, 5, 6, 7),
        scratch=[
            tiles, pltpu.VMEM((length, 2 * head), BF16), pltpu.SemaphoreType.DMA((2 * len(SIZES),))
        ],
        flops=2 * length * width * 4 * head,
    )(info, weight, table, mask, *early, *later, *pieces[len(SIZES) :])
    attended_own = exchange(attended)

    row_shape = shape((rows, width), BF16)
    send, gate_grad, gated = call(
        mix_kernel,
        [shape((heads, rows, 2 * head), BF16), row_shape, row_shape],
        "mix",
    )(attended_own, gate_proj, gg)
    mix_head = exchange(send)

    grads = call(
        functools.partial(backward_kernel, scale),
        [shape((8, rows, 3 * head), BF16)],
        "backward",
        parts={1: 4, 2: 4, 3: 4},
        out_parts={0: 2},
        scratch=[
            pltpu.VMEM((length, head), F32),
            pltpu.VMEM((length, head), F32),
            tiles,
            pltpu.VMEM((length, 2 * head), BF16),
        ],
        flops=10 * length * 4096 * head,
    )(table, mask, features, mix_head, slopes)[0]
    grads_own = exchange(grads)

    cells = shape((8, width // 16, 4 * head + width), BF16)
    third = shape((8, width // 16, 4 * head), BF16)
    mine, first, second, last = call(
        sums_kernel,
        [cells, third, third, third],
        "sums",
        smem=1,
        scratch=[pltpu.VMEM((length, 4 * head), BF16)],
        flops=2 * length * width * 4 * head + 2 * rows * width * width,
    )(info, mix_head, grads, *pieces, gated, upstream)
    others = [swap(part, "dp", 1, 16) for part in (first, second, last)]
    both = call(join_kernel, [cells], "join", light=True, limit=16)(mine, *others)[0]
    both, grads_own = lax.optimization_barrier((both, grads_own))
    few = width // 128
    parts = exchange_chips(both.reshape(64, few, 4 * head + width))
    final = jnp.sum(parts.reshape(8, 8, few, -1).astype(F32), axis=0)
    proj_out = final[:, :, : 4 * head].reshape(8, few, 4, head)
    proj_out = proj_out.transpose(1, 2, 0, 3).reshape(few, 4 * width)
    out_out = jnp.sum(final[:, :, 4 * head :], axis=0)

    grad_row, layer_row = call(
        input_kernel,
        [row_shape, row_shape],
        "input_grad",
        parts={2: width // TILE},
        scratch=[pltpu.VMEM((rows, 4 * width), BF16), pltpu.VMEM((rows, width), F32)],
        flops=8 * rows * width * width,
    )(gate_grad, grads_own, proj_weight, token_row, upstream, gated, out_weight)
    return layer_row[None], grad_row[None], proj_out, out_out


def solution(mesh):
    return jax.shard_map(
        per_device,
        mesh=mesh,
        in_specs=(P("dp", "seq", None), P(), P(), P(), P("dp", None), P(), P("dp", "seq", None)),
        out_specs=(
            P("dp", "seq", None),
            P("dp", "seq", None),
            P(("dp", "seq"), None),
            P(("dp", "seq"), None),
        ),
        check_vma=False,
    )
```
